256 devices in a mesh: qrow: 16 (over z_lo, x), kcol: 16 (over z_hi, y, core).
Axes of the slice: x: 4, y: 4, z: 8 (z_hi: 2, z_lo: 4; z = z_hi * 4 + z_lo), core: 2. Of those that a mesh axis runs over, the one named last changes fastest.
Arguments:
- queries: bfloat16 [1024, 8192], P(('qrow', 'kcol')), may hold values from -200 to 200
- keys_values: bfloat16 [2, 32768, 512], P(None, ('kcol', 'qrow')), may hold values from -8 to 8
- doc_blocks: int32 [256], replicated, may hold values from 0 to 11, never falling along the last dimension, each value on 1 to 129 neighbouring positions
Outputs:
- attended: bfloat16 [1024, 8192], P(('qrow', 'kcol'))
The draws below stay inside these ranges and needn't reach their ends.
Inputs may be any that keep to these rules, and one draw needn't show every extreme that they name: doc_blocks[b] is the document of positions 128 b to 128 b + 127; each document covers 1 to 129 consecutive entries (blocks), one document exactly that many.
All inputs are finite; a program needn't handle non-finite values.
Results may differ from the reference program's by a relative error of at most 0.0046.
Values may be sent and summed in bfloat16 or wider, within the bound.
No kernel may reach another device: no remote copies, remote signals or barrier semaphores. Data moves between devices by JAX's collectives and lax.ppermute only.
A program may use at most 128 MiB of HBM per device.

```python
import math
import jax
import jax.numpy as jnp
import numpy as np
from jax import lax

QUERY_HEADS = 64
KEY_VALUE_HEADS = 4
HEAD_WIDTH = 128
TQ = 1024
TOTAL_KEY_COUNT = 32768
STRIPE = 4096
KBLK = 256
DOCS = 12
N_KCOL = 16


def base_keys(key):
    return jax.random.truncated_normal(jax.random.fold_in(key, 11), -6.0, 6.0, (TOTAL_KEY_COUNT, KEY_VALUE_HEADS * HEAD_WIDTH), jnp.float32)


def draw_queries(key, part):
    shape_all = (TQ, QUERY_HEADS * HEAD_WIDTH)
    return jax.random.truncated_normal(jax.random.fold_in(key, 23), -6.0, 6.0, shape_all, jnp.float32).astype(jnp.bfloat16)


def draw_keys_values(key, part):
    key_matrix_rows = base_keys(key)
    value_matrix_rows = jax.random.truncated_normal(jax.random.fold_in(key, 37), -6.0, 6.0, (TOTAL_KEY_COUNT, KEY_VALUE_HEADS * HEAD_WIDTH), jnp.float32)
    return jnp.stack([key_matrix_rows, value_matrix_rows]).astype(jnp.bfloat16)


def split_up(amount, total, reach, slope):
    loads = [(1 << 20) // math.isqrt(grade ** slope) + 1 for grade in range(2, amount + 1)]
    surplus, counts = total - reach - (amount - 1), [1] * (amount - 1)
    while surplus > 0:
        candidates = [i for i in range(amount - 1) if counts[i] < reach]
        whole, left = sum([loads[i] for i in candidates]), surplus
        for i in candidates:
            addition = min(reach - counts[i], max(1, left * loads[i] // whole), surplus)
            counts[i] = counts[i] + addition
            surplus = surplus - addition
    return np.array([reach] + counts)


def ragged(own_key, amount, total, most, lean):
    if amount == 2:
        one = jax.random.randint(own_key, (), max(1, total - most), min(most, total - 1) + 1)
        return jnp.stack([one, total - one])
    tallies = jnp.asarray(split_up(amount, total, most, lean), jnp.int32)
    pairs = (amount - 1) // 2
    giver, sink = tallies[1:1 + 2 * pairs:2], tallies[2:2 + 2 * pairs:2]
    margin = jnp.minimum(giver - 1, most - sink)
    moved = jax.random.randint(jax.random.fold_in(own_key, 1), (pairs,), 0, 1 << 20) % (margin + 1)
    tallies = tallies.at[1:1 + 2 * pairs:2].set(giver - moved).at[2:2 + 2 * pairs:2].set(sink + moved)
    return tallies[jax.random.permutation(jax.random.fold_in(own_key, 2), amount)]


def setup_inputs(seed: int = 0) -> dict:
    key_of = jax.random.split(jax.random.key(seed), 4)
    queries = draw_queries(jax.random.fold_in(key_of[3], 71), 0)
    keys_values = draw_keys_values(jax.random.fold_in(key_of[3], 71), 0)
    doc_blocks = jnp.searchsorted(jnp.cumsum(ragged(key_of[2], DOCS, KBLK, KBLK // 2 + 1, 2)), jnp.arange(KBLK), side="right").astype(jnp.int32)
    return {"queries": queries, "keys_values": keys_values, "doc_blocks": doc_blocks}


masked_score = -1e+30

def reference(queries, keys_values, doc_blocks):
    query_group_width = QUERY_HEADS // KEY_VALUE_HEADS
    range_keys = TOTAL_KEY_COUNT // N_KCOL
    score_scale = 1.0 / math.sqrt(HEAD_WIDTH)
    key_pos = jnp.arange(TOTAL_KEY_COUNT, dtype=jnp.int32)
    key_doc = jnp.repeat(doc_blocks, 128)
    key_matrix_rows = keys_values[0].astype(jnp.float32)
    value_matrix_rows = keys_values[1].astype(jnp.float32)

    def one_block(block_index):
        block_index = block_index.astype(jnp.int32)
        first_row = block_index * 128
        query_rows = lax.dynamic_slice_in_dim(queries, first_row, 128, 0).astype(jnp.float32)
        query_pos = block_index * STRIPE + STRIPE - 128 + jnp.arange(128, dtype=jnp.int32)
        query_doc = doc_blocks[block_index * (STRIPE // 128) + STRIPE // 128 - 1]
        live_mask = (key_doc[None, :] == query_doc) & (key_pos[None, :] <= query_pos[:, None])
        ranged_mask = live_mask.reshape(1, 128, N_KCOL, range_keys)
        head_outputs = []
        for query_head_group in range(KEY_VALUE_HEADS):
            grouped = query_rows[:, query_head_group * query_group_width * HEAD_WIDTH:(query_head_group + 1) * query_group_width * HEAD_WIDTH].reshape(128, query_group_width, HEAD_WIDTH)
            key_part = key_matrix_rows[:, query_head_group * HEAD_WIDTH:(query_head_group + 1) * HEAD_WIDTH]
            value_part = value_matrix_rows[:, query_head_group * HEAD_WIDTH:(query_head_group + 1) * HEAD_WIDTH].reshape(N_KCOL, range_keys, HEAD_WIDTH)
            scores = jnp.einsum('qhd,kd->hqk', grouped, key_part) * score_scale
            scores = jnp.where(live_mask[None], scores, masked_score).reshape(query_group_width, 128, N_KCOL, range_keys)
            range_max = lax.optimization_barrier(jnp.max(scores, axis=3))
            weights = jnp.where(ranged_mask, jnp.exp(scores - range_max[..., None]), 0.0)
            range_sum = lax.optimization_barrier(jnp.sum(weights, axis=3))
            rounded = lax.optimization_barrier(weights.astype(jnp.bfloat16)).astype(jnp.float32)
            range_out = jnp.einsum('hqrk,rkd->hqrd', rounded, value_part)
            overall = lax.optimization_barrier(jnp.max(range_max, axis=2))
            factor = jnp.exp(range_max - overall[..., None])
            total_out = lax.optimization_barrier(jnp.sum(range_out * factor[..., None], axis=2))
            total_sum = lax.optimization_barrier(jnp.sum(range_sum * factor, axis=2))
            head_outputs.append(total_out / total_sum[..., None])
        joined = jnp.concatenate(head_outputs, axis=0)
        return jnp.transpose(joined, (1, 0, 2)).reshape(128, QUERY_HEADS * HEAD_WIDTH).astype(jnp.bfloat16)
    blocks = lax.map(one_block, jnp.arange(TQ // 128, dtype=jnp.int32))
    return blocks.reshape(TQ, QUERY_HEADS * HEAD_WIDTH)
```

```python
import functools
import math

import jax
import jax.numpy as jnp
from jax import lax
from jax.experimental import pallas as pl
from jax.experimental.pallas import tpu as pltpu
from jax.sharding import Mesh
from jax.sharding import PartitionSpec as P

HEADS = 64
GROUPS = 4
WIDTH = 128
BLOCK = 128
HEADS_PER_GROUP = HEADS // GROUPS
MASKED = -1e30
EXP_SCALE = math.log2(math.e) / math.sqrt(WIDTH)
SLOT_ROWS = 80
VMEM = pl.BlockSpec(memory_space=pltpu.VMEM)
SMEM = pl.BlockSpec(memory_space=pltpu.SMEM)


def three_pieces(value):
    hi = value.astype(jnp.bfloat16).astype(jnp.float32)
    rest = value - hi
    mid = rest.astype(jnp.bfloat16).astype(jnp.float32)
    return hi, mid, rest - mid


def attend(scal, q_ref, a0, a1, a2, a3, b0, b1, out_ref, s_scr, p_scr, acc, m_scr, l_scr):
    zl, x, core, x0 = scal[8], scal[9], scal[10], scal[11]
    own = (a0, a1, a2, a3)

    def block(crel, xr, s, which):
        if crel == 0:
            return own[xr][s, which]
        half = b0 if xr < 2 else b1
        return half[(xr % 2) * 4 + s, which]

    for group in range(4):
        lo, hi, diagonal = scal[group], scal[4 + group], scal[12 + group]
        rows = pl.ds(group * 512, 512)

        @pl.when(lo < hi)
        def _():
            m_scr[...] = jnp.full_like(m_scr, MASKED)
            l_scr[...] = jnp.zeros_like(l_scr)
            acc[...] = jnp.zeros_like(acc)
            for crel in range(2):
                c_at = core ^ crel
                first = jnp.clip(lo - 16 * c_at, 0, 16)
                last = jnp.clip(hi - 16 * c_at, 0, 16)

                def chunk(zl_at, carry, crel=crel, c_at=c_at):
                    s = zl_at ^ zl
                    keys = jnp.concatenate([block(crel, xr, s, 0) for xr in range(4)], axis=0)
                    s_scr[...] = lax.dot_general(
                        keys,
                        q_ref[rows, :],
                        (((1,), (1,)), ((), ())),
                        preferred_element_type=jnp.float32,
                    )
                    base = c_at * 16 + zl_at * 4

                    @pl.when((diagonal >= base) & (diagonal < base + 4))
                    def _():
                        at = pl.ds(pl.multiple_of(((diagonal - base - x) & 3) * 128, 128), 128)
                        key = lax.broadcasted_iota(jnp.int32, (128, 512), 0)
                        row = lax.broadcasted_iota(jnp.int32, (128, 512), 1)
                        query = x0 * 64 + (row >> 6) * 8 + core * 4 + (row & 3)
                        s_scr[at, :] = jnp.where(key <= query, s_scr[at, :], MASKED)

                    m_old = m_scr[0:1, :]
                    m_new = m_old
                    bias = []
                    for xr in range(4):
                        at = base + ((x + xr) & 3)
                        dead = (at < lo) | (at >= hi)
                        bias.append(jnp.where(dead, jnp.float32(MASKED), jnp.float32(0.0)))
                        top = jnp.max(s_scr[xr * 128 : (xr + 1) * 128, :], axis=0, keepdims=True)
                        m_new = jnp.maximum(m_new, top + bias[xr])
                    total = jnp.zeros((1, 512), jnp.float32)
                    for xr in range(4):
                        at = slice(xr * 128, (xr + 1) * 128)
                        p = jnp.exp2((s_scr[at, :] - (m_new - bias[xr])) * EXP_SCALE)
                        total = total + jnp.sum(p, axis=0, keepdims=True)
                        p_scr[at, :] = p.astype(jnp.bfloat16)
                    alpha = jnp.exp2((m_old - m_new) * EXP_SCALE)
                    m_scr[0:1, :] = m_new
                    l_scr[0:1, :] = l_scr[0:1, :] * alpha + total
                    values = jnp.concatenate([block(crel, xr, s, 1) for xr in range(4)], axis=0)
                    acc[...] = acc[...] * alpha + lax.dot_general(
                        values,
                        p_scr[...],
                        (((0,), (0,)), ((), ())),
                        preferred_element_type=jnp.float32,
                    )
                    return carry

                lax.fori_loop(first // 4, (last + 3) // 4, chunk, 0)
            part = acc[...].T.astype(jnp.bfloat16)
            stats = (*three_pieces(m_scr[0:1, :]), *three_pieces(l_scr[0:1, :]))
            stats = jnp.concatenate([*stats, jnp.zeros((10, 512), jnp.float32)], axis=0)
            stats = stats.astype(jnp.bfloat16)
            for j in range(8):
                out_ref[group * 8 + j, 0:64, :] = part[j * 64 : (j + 1) * 64]
                out_ref[group * 8 + j, 64:80, :] = stats[:, (j // 2) * 128 : (j // 2 + 1) * 128]

        @pl.when(lo >= hi)
        def _():
            row = lax.broadcasted_iota(jnp.int32, (16, 128), 0)
            stats = jnp.where(row == 0, jnp.float32(MASKED), jnp.float32(0.0)).astype(jnp.bfloat16)
            for j in range(8):
                out_ref[group * 8 + j, 0:64, :] = jnp.zeros((64, 128), jnp.bfloat16)
                out_ref[group * 8 + j, 64:80, :] = stats


def combine(scal, parts, out_ref):
    odd = scal[16] & 1
    for g in range(GROUPS):
        m, l = [], []
        for plane in range(8):
            st = parts[g * 8 + plane, 64:80, :].astype(jnp.float32)
            m.append(st[0:1] + st[1:2] + st[2:3])
            l.append(st[3:4] + st[4:5] + st[5:6])
        m, l = jnp.concatenate(m, axis=0), jnp.concatenate(l, axis=0)
        w = jnp.exp2((m - jnp.max(m, axis=0, keepdims=True)) * EXP_SCALE)
        w = w / jnp.sum(w * l, axis=0, keepdims=True)
        w = jnp.where(odd == 1, pltpu.roll(w, 64, 1), w)
        w = w.T
        total = jnp.zeros((64, 128), jnp.float32)
        for plane in range(8):
            part = parts[g * 8 + plane, 0:64, :].astype(jnp.float32)
            total = total + part * w[0:64, plane : plane + 1]
        for h in range(HEADS_PER_GROUP):
            at = (g * HEADS_PER_GROUP + h) * WIDTH
            out_ref[:, at : at + WIDTH] = total[h * 4 : (h + 1) * 4, :].astype(jnp.bfloat16)


def from_x(k):
    return [((i + k) % 4, i) for i in range(4)]


def per_device(queries, keys_values, doc_blocks):
    zl, x, zh, y, core = (lax.axis_index(a) for a in ("zl", "x", "zh", "y", "core"))
    planes = ("zl", "zh", "y")
    q = queries.reshape(4, GROUPS, HEADS_PER_GROUP, WIDTH).transpose(1, 2, 0, 3)
    q = q.reshape(GROUPS, 1, 64, WIDTH)
    q = jnp.broadcast_to(q, (GROUPS, 8, 64, WIDTH)).reshape(32, 64, WIDTH)
    q = lax.all_to_all(q, planes, 0, 0, tiled=True).reshape(2048, WIDTH)
    heads = keys_values.reshape(2, BLOCK, GROUPS, WIDTH).transpose(2, 0, 1, 3)
    pieces = [lax.dynamic_index_in_dim(heads, zl, 0, False)]
    for s in (1, 2, 3):
        piece = lax.dynamic_index_in_dim(heads, zl ^ s, 0, False)
        pieces.append(lax.ppermute(piece, "zl", [(i, i ^ s) for i in range(4)]))
    a0 = jnp.stack(pieces)
    a1, a2, a3 = (lax.ppermute(a0, "x", from_x(k)) for k in (1, 2, 3))
    swap = [(0, 1), (1, 0)]
    b0 = lax.ppermute(jnp.concatenate([a0, a1]), "core", swap)
    b1 = lax.ppermute(jnp.concatenate([a2, a3]), "core", swap)
    plane = zh * 4 + y
    query_block = 2 * jnp.arange(4, dtype=jnp.int32) + x // 2
    at = query_block * 32 + 31
    index = jnp.arange(256, dtype=jnp.int32)
    own_doc = jnp.sum(jnp.where(index[None] == at[:, None], doc_blocks[None], 0), axis=1)
    start = jnp.sum((doc_blocks[None] < own_doc[:, None]).astype(jnp.int32), axis=1)
    lo = jnp.clip(start - 32 * plane, 0, 32)
    hi = jnp.clip(at + 1 - 32 * plane, 0, 32)
    diagonal = at - 32 * plane
    mine = jnp.stack([zl, x, core, x % 2]).astype(jnp.int32)
    scal = jnp.concatenate([lo, hi, mine, diagonal, (zh * 4 + y)[None]]).astype(jnp.int32)

    part = pl.pallas_call(
        attend,
        out_shape=jax.ShapeDtypeStruct((32, SLOT_ROWS, WIDTH), jnp.bfloat16),
        in_specs=[SMEM] + [VMEM] * 7,
        out_specs=VMEM,
        scratch_shapes=[
            pltpu.VMEM((512, 512), jnp.float32),
            pltpu.VMEM((512, 512), jnp.bfloat16),
            pltpu.VMEM((WIDTH, 512), jnp.float32),
            pltpu.VMEM((8, 512), jnp.float32),
            pltpu.VMEM((8, 512), jnp.float32),
        ],
        compiler_params=pltpu.CompilerParams(vmem_limit_bytes=32 * 1024 * 1024),
        name="attend",
    )(scal, q, a0, a1, a2, a3, b0, b1)
    part = lax.all_to_all(part, planes, 0, 0, tiled=True)
    return pl.pallas_call(
        combine,
        out_shape=jax.ShapeDtypeStruct((4, HEADS * WIDTH), jnp.bfloat16),
        in_specs=[SMEM, VMEM],
        out_specs=VMEM,
        compiler_params=pltpu.CompilerParams(vmem_limit_bytes=32 * 1024 * 1024),
        name="combine",
    )(scal, part)


def solution(mesh):
    split = Mesh(mesh.devices.reshape(4, 4, 2, 4, 2), ("zl", "x", "zh", "y", "core"))
    in_specs = (
        P(("zl", "x", "zh", "y", "core"), None),
        P(None, ("zh", "y", "core", "zl", "x"), None),
        P(),
    )
    out_specs = P(("zl", "x", "zh", "y", "core"), None)
    return jax.shard_map(
        per_device, mesh=split, in_specs=in_specs, out_specs=out_specs, check_vma=False
    )
```

```python
import math

import jax
import jax.numpy as jnp
from jax import lax
from jax.experimental import pallas as pl
from jax.experimental.pallas import tpu as pltpu
from jax.sharding import Mesh
from jax.sharding import PartitionSpec as P

HEADS = 64
GROUPS = 4
BLOCK = 128
HEADS_PER_GROUP = HEADS // GROUPS
SLOT_ROWS = 80
WIDTH=128
MASKED=-1e30
EXP_SCALE = math.log2(math.e) / math.sqrt(WIDTH)
VMEM = pl.BlockSpec(memory_space=pltpu.VMEM)
SMEM = pl.BlockSpec(memory_space=pltpu.SMEM)
def three_pieces(value):
    hi = value.astype(jnp.bfloat16).astype(jnp.float32)
    rest = value - hi
    mid = rest.astype(jnp.bfloat16).astype(jnp.float32)
    return hi, mid, rest - mid

def attend_half(scal, q_ref, kv, acc, m_scr, l_scr, steps, s_a, s_b, p_a, p_b, other):
    zl, x, core, x0 = scal[8], scal[9], scal[10], scal[11]
    c_at = core ^ 1 if other else core

    def fill(n, group, zl_at, lo, hi):
        steps[0, n] = group
        steps[1, n] = zl_at
        steps[2, n] = lo
        steps[3, n] = hi

    def scores(group, zl_at, s_ref):
        s = zl_at ^ zl
        keys = jnp.concatenate([kv(xr, s, 0) for xr in range(4)], axis=0)
        q = q_ref[pl.ds(pl.multiple_of(group * 512, 512), 512), :]
        s_ref[...] = lax.dot_general(keys, q, (((1,), (1,)), ((), ())), preferred_element_type=jnp.float32)

    def softmax(group, zl_at, lo, hi, s_ref, p_ref):
        base = c_at * 16 + zl_at * 4
        m_old = m_scr[group, 0:1, :]
        m_new = m_old
        bias = []
        for xr in range(4):
            at = base + ((x + xr) & 3)
            dead = (at < lo) | (at >= hi)
            bias.append(jnp.where(dead, jnp.float32(MASKED), jnp.float32(0.0)))
            top = jnp.max(s_ref[xr * 128 : (xr + 1) * 128, :], axis=0, keepdims=True)
            m_new = jnp.maximum(m_new, top + bias[xr])
        total = jnp.zeros((1, 512), jnp.float32)
        for xr in range(4):
            at = slice(xr * 128, (xr + 1) * 128)
            p = jnp.exp2((s_ref[at, :] - (m_new - bias[xr])) * EXP_SCALE)
            total = total + jnp.sum(p, axis=0, keepdims=True)
            p_ref[at, :] = p.astype(jnp.bfloat16)
        alpha = jnp.exp2((m_old - m_new) * EXP_SCALE)
        m_scr[group, 0:1, :] = m_new
        l_scr[group, 0:1, :] = l_scr[group, 0:1, :] * alpha + total
        s = zl_at ^ zl
        values = jnp.concatenate([kv(xr, s, 1) for xr in range(4)], axis=0)
        acc[group] = acc[group] * alpha + lax.dot_general(
            values, p_ref[...], (((0,), (0,)), ((), ())), preferred_element_type=jnp.float32)

    n = jnp.int32(0)
    for group in range(4):
        lo, hi, diagonal = scal[group], scal[4 + group], scal[12 + group]
        first = jnp.clip(lo - 16 * c_at, 0, 16)
        last = jnp.clip(hi - 16 * c_at, 0, 16)
        for zl_at in range(4):
            live = (first < zl_at * 4 + 4) & (last > zl_at * 4)
            at_diagonal = live & (diagonal >> 2 == c_at * 4 + zl_at)

            @pl.when(at_diagonal)
            def _():
                scores(group, zl_at, s_a)
                slot = pl.ds(pl.multiple_of(((diagonal - x) & 3) * 128, 128), 128)
                key = lax.broadcasted_iota(jnp.int32, (128, 512), 0)
                row = lax.broadcasted_iota(jnp.int32, (128, 512), 1)
                query = x0 * 64 + (row >> 6) * 8 + core * 4 + (row & 3)
                s_a[slot, :] = jnp.where(key <= query, s_a[slot, :], MASKED)
                softmax(group, zl_at, lo, hi, s_a, p_a)

            go = live & jnp.logical_not(at_diagonal)

            @pl.when(go)
            def _(n=n):
                fill(n, group, zl_at, lo, hi)

            n = n + go.astype(jnp.int32)

    @pl.when(n > 0)
    def _():
        for k in range(2):
            fill(n + k, steps[0, n - 1], steps[1, n - 1], 0, 0)

        def get(i):
            return steps[0, i], steps[1, i], steps[2, i], steps[3, i]

        g, z, _, _ = get(0)
        scores(g, z, s_a)

        def pair(i, carry):
            one, two, three = get(2 * i), get(2 * i + 1), get(2 * i + 2)
            scores(*two[:2], s_b)
            softmax(*one, s_a, p_a)
            scores(*three[:2], s_a)
            softmax(*two, s_b, p_b)
            return carry

        lax.fori_loop(0, (n + 1) // 2, pair, 0)

def attend_own(scal, q_ref, a0, a1, a2, a3, acc, m_scr, l_scr, steps, s_a, s_b, p_a, p_b):
    own = (a0, a1, a2, a3)
    m_scr[...] = jnp.full_like(m_scr, MASKED)
    l_scr[...] = jnp.zeros_like(l_scr)
    acc[...] = jnp.zeros_like(acc)
    attend_half(scal, q_ref, lambda xr, s, w: own[xr][s, w], acc, m_scr, l_scr, steps, s_a, s_b, p_a, p_b, False)

def attend_other(scal, q_ref, b0, b1, acc_in, m_in, l_in, out_ref, acc, m_scr, l_scr, steps, s_a, s_b, p_a, p_b):
    both = (b0, b1)
    m_scr[...] = m_in[...]
    l_scr[...] = l_in[...]
    acc[...] = acc_in[...]
    attend_half(scal, q_ref, lambda xr, s, w: both[xr // 2][(xr % 2) * 4 + s, w], acc, m_scr, l_scr, steps, s_a, s_b, p_a, p_b, True)
    for group in range(4):
        lo, hi = scal[group], scal[4 + group]

        @pl.when(lo < hi)
        def _():
            part = acc[group].T.astype(jnp.bfloat16)
            stats = (*three_pieces(m_scr[group, 0:1, :]), *three_pieces(l_scr[group, 0:1, :]))
            stats = jnp.concatenate([*stats, jnp.zeros((10, 512), jnp.float32)], axis=0)
            stats = stats.astype(jnp.bfloat16)
            for j in range(8):
                out_ref[group * 8 + j, 0:64, :] = part[j * 64 : (j + 1) * 64]
                out_ref[group * 8 + j, 64:80, :] = stats[:, (j // 2) * 128 : (j // 2 + 1) * 128]

        @pl.when(lo >= hi)
        def _():
            row = lax.broadcasted_iota(jnp.int32, (16, 128), 0)
            stats = jnp.where(row == 0, jnp.float32(MASKED), jnp.float32(0.0)).astype(jnp.bfloat16)
            for j in range(8):
                out_ref[group * 8 + j, 0:64, :] = jnp.zeros((64, 128), jnp.bfloat16)
                out_ref[group * 8 + j, 64:80, :] = stats
STATE=(jax.ShapeDtypeStruct((4,128,512),jnp.float32),jax.ShapeDtypeStruct((4,8,512),jnp.float32),jax.ShapeDtypeStruct((4,8,512),jnp.float32))
SCR=[pltpu.SMEM((4,32),jnp.int32),pltpu.VMEM((512,512),jnp.float32),pltpu.VMEM((512,512),jnp.float32),pltpu.VMEM((512,512),jnp.bfloat16),pltpu.VMEM((512,512),jnp.bfloat16)]
CP=pltpu.CompilerParams(vmem_limit_bytes=32*1024*1024)
COST=pl.CostEstimate(flops=2*2*1024*2048*128,bytes_accessed=4<<20,transcendentals=1024*2048)
def own_call(scal,q,a0,a1,a2,a3):
    return pl.pallas_call(attend_own,out_shape=STATE,in_specs=[SMEM]+[VMEM]*5,out_specs=(VMEM,)*3,scratch_shapes=SCR,compiler_params=CP,cost_estimate=COST,name="attend_own")(scal,q,a0,a1,a2,a3)
def other_call(scal,q,b0,b1,*state):
    return pl.pallas_call(attend_other,out_shape=jax.ShapeDtypeStruct((32,80,128),jnp.bfloat16),in_specs=[SMEM]+[VMEM]*6,out_specs=VMEM,
      scratch_shapes=[pltpu.VMEM(s.shape,s.dtype) for s in STATE]+SCR,compiler_params=CP,cost_estimate=COST,name="attend_other")(scal,q,b0,b1,*state)


def combine(scal, parts, out_ref):
    odd = scal[16] & 1
    for g in range(GROUPS):
        m, l = [], []
        for plane in range(8):
            st = parts[g * 8 + plane, 64:80, :].astype(jnp.float32)
            m.append(st[0:1] + st[1:2] + st[2:3])
            l.append(st[3:4] + st[4:5] + st[5:6])
        m, l = jnp.concatenate(m, axis=0), jnp.concatenate(l, axis=0)
        w = jnp.exp2((m - jnp.max(m, axis=0, keepdims=True)) * EXP_SCALE)
        w = w / jnp.sum(w * l, axis=0, keepdims=True)
        w = jnp.where(odd == 1, pltpu.roll(w, 64, 1), w)
        w = w.T
        total = jnp.zeros((64, 128), jnp.float32)
        for plane in range(8):
            part = parts[g * 8 + plane, 0:64, :].astype(jnp.float32)
            total = total + part * w[0:64, plane : plane + 1]
        for h in range(HEADS_PER_GROUP):
            at = (g * HEADS_PER_GROUP + h) * WIDTH
            out_ref[:, at : at + WIDTH] = total[h * 4 : (h + 1) * 4, :].astype(jnp.bfloat16)


def from_x(k):
    return [((i + k) % 4, i) for i in range(4)]


def per_device(queries, keys_values, doc_blocks):
    zl, x, zh, y, core = (lax.axis_index(a) for a in ("zl", "x", "zh", "y", "core"))
    planes = ("zl", "zh", "y")
    q = queries.reshape(4, GROUPS, HEADS_PER_GROUP, WIDTH).transpose(1, 2, 0, 3)
    q = q.reshape(GROUPS, 1, 64, WIDTH)
    q = jnp.broadcast_to(q, (GROUPS, 8, 64, WIDTH)).reshape(32, 64, WIDTH)
    q = lax.all_to_all(q, planes, 0, 0, tiled=True).reshape(2048, WIDTH)
    heads = keys_values.reshape(2, BLOCK, GROUPS, WIDTH).transpose(2, 0, 1, 3)
    pieces = [lax.dynamic_index_in_dim(heads, zl, 0, False)]
    for s in (1, 2, 3):
        piece = lax.dynamic_index_in_dim(heads, zl ^ s, 0, False)
        pieces.append(lax.ppermute(piece, "zl", [(i, i ^ s) for i in range(4)]))
    a0 = jnp.stack(pieces)
    a1, a2, a3 = (lax.ppermute(a0, "x", from_x(k)) for k in (1, 2, 3))
    swap = [(0, 1), (1, 0)]
    b0 = lax.ppermute(jnp.concatenate([a0, a1]), "core", swap)
    b1 = lax.ppermute(jnp.concatenate([a2, a3]), "core", swap)
    plane = zh * 4 + y
    query_block = 2 * jnp.arange(4, dtype=jnp.int32) + x // 2
    at = query_block * 32 + 31
    index = jnp.arange(256, dtype=jnp.int32)
    own_doc = jnp.sum(jnp.where(index[None] == at[:, None], doc_blocks[None], 0), axis=1)
    start = jnp.sum((doc_blocks[None] < own_doc[:, None]).astype(jnp.int32), axis=1)
    lo = jnp.clip(start - 32 * plane, 0, 32)
    hi = jnp.clip(at + 1 - 32 * plane, 0, 32)
    diagonal = at - 32 * plane
    mine = jnp.stack([zl, x, core, x % 2]).astype(jnp.int32)
    scal = jnp.concatenate([lo, hi, mine, diagonal, (zh * 4 + y)[None]]).astype(jnp.int32)

    state = own_call(scal, q, a0, a1, a2, a3)
    part = other_call(scal, q, b0, b1, *state)
    part = lax.all_to_all(part, planes, 0, 0, tiled=True)
    return pl.pallas_call(
        combine,
        out_shape=jax.ShapeDtypeStruct((4, HEADS * WIDTH), jnp.bfloat16),
        in_specs=[SMEM, VMEM],
        out_specs=VMEM,
        compiler_params=CP,
        name="combine",
    )(scal, part)


def solution(mesh):
    split = Mesh(mesh.devices.reshape(4, 4, 2, 4, 2), ("zl", "x", "zh", "y", "core"))
    in_specs = (
        P(("zl", "x", "zh", "y", "core"), None),
        P(None, ("zh", "y", "core", "zl", "x"), None),
        P(),
    )
    out_specs = P(("zl", "x", "zh", "y", "core"), None)
    return jax.shard_map(
        per_device, mesh=split, in_specs=in_specs, out_specs=out_specs, check_vma=False
    )
```

```python
import math

import jax
import jax.numpy as jnp
from jax import lax
from jax.experimental import pallas as pl
from jax.experimental.pallas import tpu as pltpu
from jax.sharding import Mesh
from jax.sharding import PartitionSpec as P

HEADS = 64
GROUPS = 4
WIDTH = 128
BLOCK = 128
HEADS_PER_GROUP = HEADS // GROUPS
SLOT_ROWS = 80
ROWS = 256
KEYS = 512
MASKED = -1e30
EXP_SCALE = math.log2(math.e) / math.sqrt(WIDTH)
VMEM = pl.BlockSpec(memory_space=pltpu.VMEM)
SMEM = pl.BlockSpec(memory_space=pltpu.SMEM)
PARAMS = pltpu.CompilerParams(vmem_limit_bytes=32 * 1024 * 1024)


def three_pieces(value):
    hi = value.astype(jnp.bfloat16).astype(jnp.float32)
    rest = value - hi
    mid = rest.astype(jnp.bfloat16).astype(jnp.float32)
    return hi, mid, rest - mid


def attend(
    scal, q_ref, a0, a1, a2, a3, b0, b1, out_ref,
    k_scr, v_scr, acc, m_scr, l_scr, steps, s_a, s_b, p_a, p_b,
):
    zl, y, core, causal = scal[16], scal[17], scal[18], scal[19]
    for k in range(4):
        own, half = (a0, a1, a2, a3)[k], (b0, b1)[k // 2]
        for s in range(4):
            at = ((y + k) & 3) * 8 + (s ^ zl)
            for src, j, p in ((own, s, at + core * 4), (half, k % 2 * 4 + s, at + (core ^ 1) * 4)):
                rows = pl.ds(pl.multiple_of(p * BLOCK, BLOCK), BLOCK)
                k_scr[rows, :] = src[j, 0]
                v_scr[rows, :] = src[j, 1]
    m_scr[...] = jnp.full_like(m_scr, MASKED)
    l_scr[...] = jnp.zeros_like(l_scr)

    def put(n, group, start, lo, slack):
        steps[0, n] = group
        steps[1, n] = start
        steps[2, n] = lo
        steps[3, n] = slack

    def plan(group, n):
        lo, hi = scal[group], scal[8 + group]
        count = (jnp.maximum(hi - lo, 0) + 3) // 4

        @pl.when(count > 0)
        def _():
            acc[group] = jnp.zeros((WIDTH, ROWS), jnp.float32)

        def one(i, n):
            diagonal = (i == 0) & (causal == 1) & (hi == scal[20 + group])
            put(n, group, hi - 4 - 4 * i, lo, jnp.where(diagonal, 0, BLOCK))
            return n + 1

        return lax.fori_loop(0, count, one, n)

    n = lax.fori_loop(0, 8, plan, jnp.int32(0))
    key = lax.broadcasted_iota(jnp.int32, (BLOCK, ROWS), 0)
    row = lax.broadcasted_iota(jnp.int32, (1, ROWS), 1)
    query = (row >> 7) * 64 + ((row >> 6) & 1) * 32 + y * 8 + core * 4 + (row & 3)

    def scores(i, s_ref):
        group, start = steps[0, i], steps[1, i]
        keys = k_scr[pl.ds(pl.multiple_of(start * BLOCK, KEYS), KEYS), :]
        q = q_ref[pl.ds(pl.multiple_of(group * ROWS, ROWS), ROWS), :]
        s_ref[...] = lax.dot_general(
            keys, q, (((1,), (1,)), ((), ())), preferred_element_type=jnp.float32
        )

    def weigh(i, s_ref, p_ref):
        group, start, lo, slack = steps[0, i], steps[1, i], steps[2, i], steps[3, i]
        tail = slice(3 * BLOCK, KEYS)
        s_ref[tail, :] = jnp.where(key <= query + slack, s_ref[tail, :], MASKED)
        m_old = m_scr[group, 0:1, :]
        m_new = m_old
        bias = []
        for j in range(4):
            bias.append(jnp.where(start + j < lo, jnp.float32(MASKED), jnp.float32(0.0)))
            top = jnp.max(s_ref[j * BLOCK : (j + 1) * BLOCK, :], axis=0, keepdims=True)
            m_new = jnp.maximum(m_new, top + bias[j])
        total = jnp.zeros((1, ROWS), jnp.float32)
        for j in range(4):
            at = slice(j * BLOCK, (j + 1) * BLOCK)
            p = jnp.exp2((s_ref[at, :] - (m_new - bias[j])) * EXP_SCALE)
            total = total + jnp.sum(p, axis=0, keepdims=True)
            p_ref[at, :] = p.astype(jnp.bfloat16)
        alpha = jnp.exp2((m_old - m_new) * EXP_SCALE)
        m_scr[group, 0:1, :] = m_new
        l_scr[group, 0:1, :] = l_scr[group, 0:1, :] * alpha + total
        values = v_scr[pl.ds(pl.multiple_of(start * BLOCK, KEYS), KEYS), :]
        acc[group] = acc[group] * alpha + lax.dot_general(
            values, p_ref[...], (((0,), (0,)), ((), ())), preferred_element_type=jnp.float32
        )

    @pl.when(n > 0)
    def _():
        for extra in range(2):
            put(n + extra, steps[0, n - 1], steps[1, n - 1], 64, BLOCK)
        scores(0, s_a)

        def pair(i, carry):
            scores(2 * i + 1, s_b)
            weigh(2 * i, s_a, p_a)
            scores(2 * i + 2, s_a)
            weigh(2 * i + 1, s_b, p_b)
            return carry

        lax.fori_loop(0, (n + 1) // 2, pair, 0)

    def finish(group, carry):
        live = scal[group] < scal[8 + group]

        @pl.when(live)
        def _():
            part = acc[group].T.astype(jnp.bfloat16)
            for j in range(4):
                out_ref[group * 4 + j, 0:64, :] = part[j * 64 : (j + 1) * 64]

        @pl.when(jnp.logical_not(live))
        def _():
            for j in range(4):
                out_ref[group * 4 + j, 0:64, :] = jnp.zeros((64, WIDTH), jnp.bfloat16)

        stats = (*three_pieces(m_scr[group, 0:1, :]), *three_pieces(l_scr[group, 0:1, :]))
        stats = jnp.concatenate([*stats, jnp.zeros((10, ROWS), jnp.float32)], axis=0)
        stats = stats.astype(jnp.bfloat16)
        for j in range(4):
            out_ref[group * 4 + j, 64:80, :] = stats[:, j // 2 * 128 : (j // 2 + 1) * 128]
        return carry

    lax.fori_loop(0, 8, finish, 0)


def attend_call(scal, q, a, b):
    return pl.pallas_call(
        attend,
        out_shape=jax.ShapeDtypeStruct((32, SLOT_ROWS, WIDTH), jnp.bfloat16),
        in_specs=[SMEM] + [VMEM] * 7,
        out_specs=VMEM,
        scratch_shapes=[
            pltpu.VMEM((32 * BLOCK, WIDTH), jnp.bfloat16),
            pltpu.VMEM((32 * BLOCK, WIDTH), jnp.bfloat16),
            pltpu.VMEM((8, WIDTH, ROWS), jnp.float32),
            pltpu.VMEM((8, 8, ROWS), jnp.float32),
            pltpu.VMEM((8, 8, ROWS), jnp.float32),
            pltpu.SMEM((4, 72), jnp.int32),
            pltpu.VMEM((KEYS, ROWS), jnp.float32),
            pltpu.VMEM((KEYS, ROWS), jnp.float32),
            pltpu.VMEM((KEYS, ROWS), jnp.bfloat16),
            pltpu.VMEM((KEYS, ROWS), jnp.bfloat16),
        ],
        compiler_params=PARAMS,
        name="attend",
    )(scal, q, *a, *b)


def combine(scal, parts, out_ref):
    odd = scal[28]
    for g in range(GROUPS):
        m, l = [], []
        for plane in range(8):
            st = parts[g * 8 + plane, 64:80, :].astype(jnp.float32)
            m.append(st[0:1] + st[1:2] + st[2:3])
            l.append(st[3:4] + st[4:5] + st[5:6])
        m, l = jnp.concatenate(m, axis=0), jnp.concatenate(l, axis=0)
        w = jnp.exp2((m - jnp.max(m, axis=0, keepdims=True)) * EXP_SCALE)
        w = w / jnp.sum(w * l, axis=0, keepdims=True)
        w = jnp.where(odd == 1, pltpu.roll(w, 64, 1), w)
        w = w.T
        total = jnp.zeros((64, 128), jnp.float32)
        for plane in range(8):
            part = parts[g * 8 + plane, 0:64, :].astype(jnp.float32)
            total = total + part * w[0:64, plane : plane + 1]
        for h in range(HEADS_PER_GROUP):
            at = (g * HEADS_PER_GROUP + h) * WIDTH
            out_ref[:, at : at + WIDTH] = total[h * 4 : (h + 1) * 4, :].astype(jnp.bfloat16)


def turned(k):
    return [((i + k) % 4, i) for i in range(4)]


def per_device(queries, keys_values, doc_blocks):
    zl, x, zh, y, core = (lax.axis_index(a) for a in ("zl", "x", "zh", "y", "core"))
    parts = ("zl", "x", "zh")
    q = queries.reshape(4, GROUPS, HEADS_PER_GROUP, WIDTH).transpose(1, 2, 0, 3)
    q = q.reshape(GROUPS, 1, 64, WIDTH)
    q = jnp.broadcast_to(q, (GROUPS, 8, 64, WIDTH)).reshape(32, 64, WIDTH)
    q = lax.all_to_all(q, parts, 0, 0, tiled=True).reshape(2048, WIDTH)
    pieces = []
    for s in range(4):
        piece = lax.dynamic_slice_in_dim(keys_values, (zl ^ s) * WIDTH, WIDTH, 2)
        pieces.append(lax.ppermute(piece, "zl", [(i, i ^ s) for i in range(4)]) if s else piece)
    a0 = jnp.stack(pieces)
    a1, a2, a3 = (lax.ppermute(a0, "y", turned(k)) for k in (1, 2, 3))
    swap = [(0, 1), (1, 0)]
    b = [
        lax.ppermute(jnp.concatenate(pair), "core", swap) for pair in ((a0, a1), (a2, a3))
    ]
    query_block = jnp.arange(8, dtype=jnp.int32)
    at = query_block * 32 + 31
    index = jnp.arange(256, dtype=jnp.int32)
    own_doc = jnp.sum(jnp.where(index[None] == at[:, None], doc_blocks[None], 0), axis=1)
    start = jnp.sum((doc_blocks[None] < own_doc[:, None]).astype(jnp.int32), axis=1)
    lo = jnp.clip((start - x - 128 * zh + 3) >> 2, 0, 32)
    end = 8 * (query_block + 1) - 32 * zh
    mine = jnp.stack([zl, y, core, (x == 3).astype(jnp.int32)]).astype(jnp.int32)
    scal = jnp.concatenate([lo, jnp.clip(end, 0, 32), mine, end, zh[None]]).astype(jnp.int32)

    part = attend_call(scal, q, (a0, a1, a2, a3), b)
    part = lax.all_to_all(part, parts, 0, 0, tiled=True)
    return pl.pallas_call(
        combine,
        out_shape=jax.ShapeDtypeStruct((4, HEADS * WIDTH), jnp.bfloat16),
        in_specs=[SMEM, VMEM],
        out_specs=VMEM,
        compiler_params=PARAMS,
        name="combine",
    )(scal, part)


def solution(mesh):
    split = Mesh(mesh.devices.reshape(4, 4, 2, 4, 2), ("zl", "x", "zh", "y", "core"))
    in_specs = (
        P(("zl", "x", "zh", "y", "core"), None),
        P(None, ("zh", "y", "core", "zl", "x"), None),
        P(),
    )
    out_specs = P(("zl", "x", "zh", "y", "core"), None)
    return jax.shard_map(
        per_device, mesh=split, in_specs=in_specs, out_specs=out_specs, check_vma=False
    )
```

```python
import math

import jax
import jax.numpy as jnp
from jax import lax
from jax.experimental import pallas as pl
from jax.experimental.pallas import tpu as pltpu
from jax.sharding import Mesh
from jax.sharding import PartitionSpec as P

HEADS = 64
GROUPS = 4
WIDTH = 128
BLOCK = 128
HEADS_PER_GROUP = HEADS // GROUPS
SLOT_ROWS = 72
ROWS = 256
KEYS = 1024
STEP = KEYS // BLOCK
MASKED = -1e30
EXP_SCALE = math.log2(math.e) / math.sqrt(WIDTH)
VMEM = pl.BlockSpec(memory_space=pltpu.VMEM)
SMEM = pl.BlockSpec(memory_space=pltpu.SMEM)
PARAMS = pltpu.CompilerParams(vmem_limit_bytes=32 * 1024 * 1024)


def three_pieces(value):
    hi = value.astype(jnp.bfloat16).astype(jnp.float32)
    rest = value - hi
    mid = rest.astype(jnp.bfloat16).astype(jnp.float32)
    return hi, mid, rest - mid


def attend(
    scal, q_ref, a0, a1, a2, a3, b0, b1, b2, b3, out_ref,
    k_scr, v_scr, acc, m_scr, l_scr, steps, s_a, s_b, p_a, p_b,
):
    zl, y, core, causal = scal[16], scal[17], scal[18], scal[19]
    for k in range(4):
        own, other = (a0, a1, a2, a3)[k], (b0, b1, b2, b3)[k]
        for s in range(4):
            at = ((y + k) & 3) * 8 + (s ^ zl)
            for src, p in ((own, at + core * 4), (other, at + (core ^ 1) * 4)):
                rows = pl.ds(pl.multiple_of(p * BLOCK, BLOCK), BLOCK)
                k_scr[rows, :] = src[s, 0]
                v_scr[rows, :] = src[s, 1]
    m_scr[...] = jnp.full_like(m_scr, MASKED)
    l_scr[...] = jnp.zeros_like(l_scr)

    def put(n, group, start, lo, slack):
        steps[0, n] = group
        steps[1, n] = start
        steps[2, n] = lo
        steps[3, n] = slack

    def plan(group, n):
        lo, hi = scal[group], scal[8 + group]
        count = (jnp.maximum(hi - lo, 0) + STEP - 1) // STEP

        @pl.when(count > 0)
        def _():
            acc[group] = jnp.zeros((WIDTH, ROWS), jnp.float32)

        def one(i, n):
            diagonal = (i == 0) & (causal == 1) & (hi == scal[20 + group])
            put(n, group, hi - STEP - STEP * i, lo, jnp.where(diagonal, 0, BLOCK))
            return n + 1

        return lax.fori_loop(0, count, one, n)

    n = lax.fori_loop(0, 8, plan, jnp.int32(0))
    key = lax.broadcasted_iota(jnp.int32, (BLOCK, ROWS), 0)
    row = lax.broadcasted_iota(jnp.int32, (1, ROWS), 1)
    query = (row >> 7) * 64 + ((row >> 6) & 1) * 32 + y * 8 + core * 4 + (row & 3)

    def scores(i, s_ref):
        group, start = steps[0, i], steps[1, i]
        keys = k_scr[pl.ds(pl.multiple_of(start * BLOCK, KEYS), KEYS), :]
        q = q_ref[pl.ds(pl.multiple_of(group * ROWS, ROWS), ROWS), :]
        s_ref[...] = lax.dot_general(
            keys, q, (((1,), (1,)), ((), ())), preferred_element_type=jnp.float32
        )

    def weigh(i, s_ref, p_ref):
        group, start, lo, slack = steps[0, i], steps[1, i], steps[2, i], steps[3, i]
        tail = slice(KEYS - BLOCK, KEYS)
        s_ref[tail, :] = jnp.where(key <= query + slack, s_ref[tail, :], MASKED)
        m_old = m_scr[group, 0:1, :]
        m_new = m_old
        bias = []
        for j in range(STEP):
            bias.append(jnp.where(start + j < lo, jnp.float32(MASKED), jnp.float32(0.0)))
            top = jnp.max(s_ref[j * BLOCK : (j + 1) * BLOCK, :], axis=0, keepdims=True)
            m_new = jnp.maximum(m_new, top + bias[j])
        total = jnp.zeros((1, ROWS), jnp.float32)
        for j in range(STEP):
            at = slice(j * BLOCK, (j + 1) * BLOCK)
            p = jnp.exp2((s_ref[at, :] - (m_new - bias[j])) * EXP_SCALE)
            total = total + jnp.sum(p, axis=0, keepdims=True)
            p_ref[at, :] = p.astype(jnp.bfloat16)
        alpha = jnp.exp2((m_old - m_new) * EXP_SCALE)
        m_scr[group, 0:1, :] = m_new
        l_scr[group, 0:1, :] = l_scr[group, 0:1, :] * alpha + total
        values = v_scr[pl.ds(pl.multiple_of(start * BLOCK, KEYS), KEYS), :]
        acc[group] = acc[group] * alpha + lax.dot_general(
            values, p_ref[...], (((0,), (0,)), ((), ())), preferred_element_type=jnp.float32
        )

    @pl.when(n > 0)
    def _():
        for extra in range(2):
            put(n + extra, steps[0, n - 1], steps[1, n - 1], 64, BLOCK)
        scores(0, s_a)

        def pair(i, carry):
            scores(2 * i + 1, s_b)
            weigh(2 * i, s_a, p_a)
            scores(2 * i + 2, s_a)
            weigh(2 * i + 1, s_b, p_b)
            return carry

        lax.fori_loop(0, (n + 1) // 2, pair, 0)

    def finish(group, carry):
        live = scal[group] < scal[8 + group]

        @pl.when(live)
        def _():
            part = acc[group].T.astype(jnp.bfloat16)
            for j in range(4):
                out_ref[group * 4 + j, 0:64, :] = part[j * 64 : (j + 1) * 64]

        @pl.when(jnp.logical_not(live))
        def _():
            for j in range(4):
                out_ref[group * 4 + j, 0:64, :] = jnp.zeros((64, WIDTH), jnp.bfloat16)

        stats = (*three_pieces(m_scr[group, 0:1, :]), *three_pieces(l_scr[group, 0:1, :]))
        stats = jnp.concatenate([*stats, jnp.zeros((2, ROWS), jnp.float32)], axis=0)
        stats = stats.astype(jnp.bfloat16)
        for j in range(4):
            out_ref[group * 4 + j, 64:72, :] = stats[:, j // 2 * 128 : (j // 2 + 1) * 128]
        return carry

    lax.fori_loop(0, 8, finish, 0)


def attend_call(scal, q, a, b):
    return pl.pallas_call(
        attend,
        out_shape=jax.ShapeDtypeStruct((32, SLOT_ROWS, WIDTH), jnp.bfloat16),
        in_specs=[SMEM] + [VMEM] * 9,
        out_specs=VMEM,
        scratch_shapes=[
            pltpu.VMEM((32 * BLOCK, WIDTH), jnp.bfloat16),
            pltpu.VMEM((32 * BLOCK, WIDTH), jnp.bfloat16),
            pltpu.VMEM((8, WIDTH, ROWS), jnp.float32),
            pltpu.VMEM((8, 8, ROWS), jnp.float32),
            pltpu.VMEM((8, 8, ROWS), jnp.float32),
            pltpu.SMEM((4, 72), jnp.int32),
            pltpu.VMEM((KEYS, ROWS), jnp.float32),
            pltpu.VMEM((KEYS, ROWS), jnp.float32),
            pltpu.VMEM((KEYS, ROWS), jnp.bfloat16),
            pltpu.VMEM((KEYS, ROWS), jnp.bfloat16),
        ],
        compiler_params=PARAMS,
        name="attend",
    )(scal, q, *a, *b)


def combine(scal, parts, out_ref):
    odd = scal[28] == 1
    lane = lax.broadcasted_iota(jnp.int32, (1, WIDTH), 1)
    pick = lax.broadcasted_iota(jnp.int32, (64, 512), 1) & 63
    pick = pick == lax.broadcasted_iota(jnp.int32, (64, 512), 0)
    for g in range(GROUPS):
        m, l = [], []
        for part in range(8):
            st = parts[g * 8 + part, 64:72, :].astype(jnp.float32)
            m.append(st[0:1] + st[1:2] + st[2:3])
            l.append(st[3:4] + st[4:5] + st[5:6])
        m, l = jnp.concatenate(m, axis=0), jnp.concatenate(l, axis=0)
        w = jnp.exp2((m - jnp.max(m, axis=0, keepdims=True)) * EXP_SCALE)
        w = w / jnp.sum(w * l, axis=0, keepdims=True)
        turned_w = pltpu.roll(w, 64, 1)
        low, high = jnp.where(odd, turned_w, w), jnp.where(odd, w, turned_w)
        line = [jnp.where(lane < 64, low[p : p + 1], high[p + 1 : p + 2]) for p in (0, 2, 4, 6)]
        line = jnp.concatenate(line, axis=1)
        both = jnp.concatenate([parts[g * 8 + part, 0:64, :] for part in range(8)], axis=0)
        total = jnp.zeros((64, WIDTH), jnp.float32)
        for piece in three_pieces(line):
            spread = jnp.where(pick, jnp.broadcast_to(piece, (64, 512)), 0.0)
            total = total + jnp.dot(
                spread.astype(jnp.bfloat16), both, preferred_element_type=jnp.float32
            )
        for h in range(HEADS_PER_GROUP):
            at = (g * HEADS_PER_GROUP + h) * WIDTH
            out_ref[:, at : at + WIDTH] = total[h * 4 : (h + 1) * 4, :].astype(jnp.bfloat16)


def turned(k):
    return [((i + k) % 4, i) for i in range(4)]


def per_device(queries, keys_values, doc_blocks):
    zl, x, zh, y, core = (lax.axis_index(a) for a in ("zl", "x", "zh", "y", "core"))
    parts = ("zl", "x", "zh")
    q = queries.reshape(4, GROUPS, HEADS_PER_GROUP, WIDTH).transpose(1, 2, 0, 3)
    q = q.reshape(GROUPS, 1, 64, WIDTH)
    q = jnp.broadcast_to(q, (GROUPS, 8, 64, WIDTH)).reshape(32, 64, WIDTH)
    q = lax.all_to_all(q, parts, 0, 0, tiled=True).reshape(2048, WIDTH)
    pieces = []
    for s in range(4):
        piece = lax.dynamic_slice_in_dim(keys_values, (zl ^ s) * WIDTH, WIDTH, 2)
        pieces.append(lax.ppermute(piece, "zl", [(i, i ^ s) for i in range(4)]) if s else piece)
    a0 = jnp.stack(pieces)
    a1, a2, a3 = (lax.ppermute(a0, "y", turned(k)) for k in (1, 2, 3))
    swap = [(0, 1), (1, 0)]
    b0 = lax.ppermute(a0, "core", swap)
    b1 = lax.ppermute(a1, "core", swap)
    b3 = lax.ppermute(a3, "core", swap)
    a2, b3 = lax.optimization_barrier((a2, b3))
    b = [b0, b1, lax.ppermute(a2, "core", swap), b3]
    query_block = jnp.arange(8, dtype=jnp.int32)
    at = query_block * 32 + 31
    index = jnp.arange(256, dtype=jnp.int32)
    own_doc = jnp.sum(jnp.where(index[None] == at[:, None], doc_blocks[None], 0), axis=1)
    start = jnp.sum((doc_blocks[None] < own_doc[:, None]).astype(jnp.int32), axis=1)
    lo = jnp.clip((start - x - 128 * zh + 3) >> 2, 0, 32)
    end = 8 * (query_block + 1) - 32 * zh
    mine = jnp.stack([zl, y, core, (x == 3).astype(jnp.int32)]).astype(jnp.int32)
    scal = jnp.concatenate([lo, jnp.clip(end, 0, 32), mine, end, zh[None]]).astype(jnp.int32)

    part = attend_call(scal, q, (a0, a1, a2, a3), b)
    part = lax.all_to_all(part, parts, 0, 0, tiled=True)
    return pl.pallas_call(
        combine,
        out_shape=jax.ShapeDtypeStruct((4, HEADS * WIDTH), jnp.bfloat16),
        in_specs=[SMEM, VMEM],
        out_specs=VMEM,
        compiler_params=PARAMS,
        name="combine",
    )(scal, part)


def solution(mesh):
    split = Mesh(mesh.devices.reshape(4, 4, 2, 4, 2), ("zl", "x", "zh", "y", "core"))
    in_specs = (
        P(("zl", "x", "zh", "y", "core"), None),
        P(None, ("zh", "y", "core", "zl", "x"), None),
        P(),
    )
    out_specs = P(("zl", "x", "zh", "y", "core"), None)
    return jax.shard_map(
        per_device, mesh=split, in_specs=in_specs, out_specs=out_specs, check_vma=False
    )
```

```python
import math

import jax
import jax.numpy as jnp
from jax import lax
from jax.experimental import pallas as pl
from jax.experimental.pallas import tpu as pltpu
from jax.sharding import Mesh
from jax.sharding import PartitionSpec as P

HEADS = 64
GROUPS = 4
WIDTH = 128
BLOCK = 128
HEADS_PER_GROUP = HEADS // GROUPS
SLOT_ROWS = 72
ROWS = 256
KEYS = 1024
STEP = KEYS // BLOCK
MASKED = -1e30
EXP_SCALE = math.log2(math.e) / math.sqrt(WIDTH)
VMEM = pl.BlockSpec(memory_space=pltpu.VMEM)
SMEM = pl.BlockSpec(memory_space=pltpu.SMEM)
PARAMS = pltpu.CompilerParams(vmem_limit_bytes=32 * 1024 * 1024)


def three_pieces(value):
    hi = value.astype(jnp.bfloat16).astype(jnp.float32)
    rest = value - hi
    mid = rest.astype(jnp.bfloat16).astype(jnp.float32)
    return hi, mid, rest - mid


def statistics(m, l):
    rows = (*three_pieces(m), *three_pieces(l), jnp.zeros((2, WIDTH), jnp.float32))
    return jnp.concatenate(rows, axis=0).astype(jnp.bfloat16)


def attend(
    scal, q0, q1, q2, q3, a0, a1, a2, a3, b0, b1, b2, b3, o0, o1, o2, o3,
    q_ref, k_scr, v_scr, acc, m_scr, l_scr, steps, s_a, s_b, p_a, p_b,
):
    zl, y, core, causal = scal[16], scal[17], scal[18], scal[19]
    for k in range(4):
        own, other = (a0, a1, a2, a3)[k], (b0, b1, b2, b3)[k]
        for s in range(4):
            at = ((y + k) & 3) * 8 + (s ^ zl)
            for src, p in ((own, at + core * 4), (other, at + (core ^ 1) * 4)):
                rows = pl.ds(pl.multiple_of(p * BLOCK, BLOCK), BLOCK)
                k_scr[rows, :] = src[s, 0]
                v_scr[rows, :] = src[s, 1]
    for k in range(4):
        x_at = (scal[29] + k) & 3
        for src in range(8):
            slot = src // 2 * 8 + x_at * 2 + src % 2
            q_ref[pl.ds(pl.multiple_of(slot * 64, 64), 64), :] = (q0, q1, q2, q3)[k][src]
    m_scr[...] = jnp.full_like(m_scr, MASKED)
    l_scr[...] = jnp.zeros_like(l_scr)

    def put(n, group, start, lo, slack):
        steps[0, n] = group
        steps[1, n] = start
        steps[2, n] = lo
        steps[3, n] = slack

    def plan(group, n):
        lo, hi = scal[group], scal[8 + group]
        count = (jnp.maximum(hi - lo, 0) + STEP - 1) // STEP

        @pl.when(count > 0)
        def _():
            acc[group] = jnp.zeros((WIDTH, ROWS), jnp.float32)

        def one(i, n):
            diagonal = (i == 0) & (causal == 1) & (hi == scal[20 + group])
            put(n, group, hi - STEP - STEP * i, lo, jnp.where(diagonal, 0, BLOCK))
            return n + 1

        return lax.fori_loop(0, count, one, n)

    n = lax.fori_loop(0, 8, plan, jnp.int32(0))
    key = lax.broadcasted_iota(jnp.int32, (BLOCK, ROWS), 0)
    row = lax.broadcasted_iota(jnp.int32, (1, ROWS), 1)
    query = (row >> 7) * 64 + ((row >> 6) & 1) * 32 + y * 8 + core * 4 + (row & 3)

    def scores(i, s_ref):
        group, start = steps[0, i], steps[1, i]
        keys = k_scr[pl.ds(pl.multiple_of(start * BLOCK, KEYS), KEYS), :]
        q = q_ref[pl.ds(pl.multiple_of(group * ROWS, ROWS), ROWS), :]
        s_ref[...] = lax.dot_general(
            keys, q, (((1,), (1,)), ((), ())), preferred_element_type=jnp.float32
        )

    def weigh(i, s_ref, p_ref):
        group, start, lo, slack = steps[0, i], steps[1, i], steps[2, i], steps[3, i]
        tail = slice(KEYS - BLOCK, KEYS)
        s_ref[tail, :] = jnp.where(key <= query + slack, s_ref[tail, :], MASKED)
        m_old = m_scr[group, 0:1, :]
        m_new = m_old
        bias = []
        for j in range(STEP):
            bias.append(jnp.where(start + j < lo, jnp.float32(MASKED), jnp.float32(0.0)))
            top = jnp.max(s_ref[j * BLOCK : (j + 1) * BLOCK, :], axis=0, keepdims=True)
            m_new = jnp.maximum(m_new, top + bias[j])
        total = jnp.zeros((1, ROWS), jnp.float32)
        for j in range(STEP):
            at = slice(j * BLOCK, (j + 1) * BLOCK)
            p = jnp.exp2((s_ref[at, :] - (m_new - bias[j])) * EXP_SCALE)
            total = total + jnp.sum(p, axis=0, keepdims=True)
            p_ref[at, :] = p.astype(jnp.bfloat16)
        alpha = jnp.exp2((m_old - m_new) * EXP_SCALE)
        m_scr[group, 0:1, :] = m_new
        l_scr[group, 0:1, :] = l_scr[group, 0:1, :] * alpha + total
        values = v_scr[pl.ds(pl.multiple_of(start * BLOCK, KEYS), KEYS), :]
        acc[group] = acc[group] * alpha + lax.dot_general(
            values, p_ref[...], (((0,), (0,)), ((), ())), preferred_element_type=jnp.float32
        )

    @pl.when(n > 0)
    def _():
        for extra in range(2):
            put(n + extra, steps[0, n - 1], steps[1, n - 1], 64, BLOCK)
        scores(0, s_a)

        def pair(i, carry):
            scores(2 * i + 1, s_b)
            weigh(2 * i, s_a, p_a)
            scores(2 * i + 2, s_a)
            weigh(2 * i + 1, s_b, p_b)
            return carry

        lax.fori_loop(0, (n + 1) // 2, pair, 0)

    for k, out_ref in enumerate((o0, o1, o2, o3)):
        x_at = (scal[29] + k) & 3
        lanes = pl.ds(pl.multiple_of((x_at & 1) * 128, 128), 128)

        def finish(zl_at, carry, out_ref=out_ref, x_at=x_at, lanes=lanes):
            group = 2 * zl_at + (x_at >> 1)
            live = scal[group] < scal[8 + group]

            @pl.when(live)
            def _():
                part = acc[group, :, lanes].T.astype(jnp.bfloat16)
                for j in range(2):
                    out_ref[zl_at * 2 + j, 0:64, :] = part[j * 64 : (j + 1) * 64]

            @pl.when(jnp.logical_not(live))
            def _():
                for j in range(2):
                    out_ref[zl_at * 2 + j, 0:64, :] = jnp.zeros((64, WIDTH), jnp.bfloat16)

            stats = statistics(m_scr[group, 0:1, lanes], l_scr[group, 0:1, lanes])
            for j in range(2):
                out_ref[zl_at * 2 + j, 64:72, :] = stats
            return carry

        lax.fori_loop(0, 4, finish, 0)


def attend_call(scal, q, a, b):
    return pl.pallas_call(
        attend,
        out_shape=(jax.ShapeDtypeStruct((8, SLOT_ROWS, WIDTH), jnp.bfloat16),) * 4,
        in_specs=[SMEM] + [VMEM] * 12,
        out_specs=(VMEM,) * 4,
        scratch_shapes=[
            pltpu.VMEM((2048, WIDTH), jnp.bfloat16),
            pltpu.VMEM((32 * BLOCK, WIDTH), jnp.bfloat16),
            pltpu.VMEM((32 * BLOCK, WIDTH), jnp.bfloat16),
            pltpu.VMEM((8, WIDTH, ROWS), jnp.float32),
            pltpu.VMEM((8, 8, ROWS), jnp.float32),
            pltpu.VMEM((8, 8, ROWS), jnp.float32),
            pltpu.SMEM((4, 72), jnp.int32),
            pltpu.VMEM((KEYS, ROWS), jnp.float32),
            pltpu.VMEM((KEYS, ROWS), jnp.float32),
            pltpu.VMEM((KEYS, ROWS), jnp.bfloat16),
            pltpu.VMEM((KEYS, ROWS), jnp.bfloat16),
        ],
        compiler_params=PARAMS,
        name="attend",
    )(scal, *q, *a, *b)


def weights(stats):
    stats = [st.astype(jnp.float32) for st in stats]
    m = jnp.concatenate([st[0:1] + st[1:2] + st[2:3] for st in stats], axis=0)
    l = jnp.concatenate([st[3:4] + st[4:5] + st[5:6] for st in stats], axis=0)
    top = jnp.max(m, axis=0, keepdims=True)
    w = jnp.exp2((m - top) * EXP_SCALE)
    return top, w, jnp.sum(w * l, axis=0, keepdims=True)


def weighed(line, pick, rows):
    total = jnp.zeros((pick.shape[0], WIDTH), jnp.float32)
    for piece in three_pieces(line):
        spread = jnp.where(pick, jnp.broadcast_to(piece, pick.shape), 0.0).astype(jnp.bfloat16)
        total = total + jnp.dot(spread, rows, preferred_element_type=jnp.float32)
    return total


def merge(p0, p1, p2, p3, out_ref):
    parts = (p0, p1, p2, p3)
    pick = lax.broadcasted_iota(jnp.int32, (128, 512), 1) & 127
    pick = pick == lax.broadcasted_iota(jnp.int32, (128, 512), 0)
    for zl_at in range(4):
        top, w, l = weights([part[2 * zl_at, 64:72, :] for part in parts])
        line = jnp.concatenate([w[k : k + 1] for k in range(4)], axis=1)
        rows = [part[2 * zl_at + j, 0:64, :] for part in parts for j in range(2)]
        total = weighed(line, pick, jnp.concatenate(rows, axis=0)).astype(jnp.bfloat16)
        stats = statistics(top, l)
        for j in range(2):
            out_ref[2 * zl_at + j, 0:64, :] = total[j * 64 : (j + 1) * 64]
            out_ref[2 * zl_at + j, 64:72, :] = stats


def combine(scal, parts, out_ref):
    odd = scal[28] == 1
    lane = lax.broadcasted_iota(jnp.int32, (1, WIDTH), 1)
    pick = lax.broadcasted_iota(jnp.int32, (64, WIDTH), 1) & 63
    pick = pick == lax.broadcasted_iota(jnp.int32, (64, WIDTH), 0)
    for g in range(GROUPS):
        _, w, l = weights([parts[g * 2 + j, 64:72, :] for j in range(2)])
        w = w / l
        turned_w = pltpu.roll(w, 64, 1)
        low, high = jnp.where(odd, turned_w, w), jnp.where(odd, w, turned_w)
        line = jnp.where(lane < 64, low[0:1], high[1:2])
        rows = jnp.concatenate([parts[g * 2 + j, 0:64, :] for j in range(2)], axis=0)
        total = weighed(line, pick, rows)
        for h in range(HEADS_PER_GROUP):
            at = (g * HEADS_PER_GROUP + h) * WIDTH
            out_ref[:, at : at + WIDTH] = total[h * 4 : (h + 1) * 4, :].astype(jnp.bfloat16)


def turned(k):
    return [((i + k) % 4, i) for i in range(4)]


def per_device(queries, keys_values, doc_blocks):
    zl, x, zh, y, core = (lax.axis_index(a) for a in ("zl", "x", "zh", "y", "core"))
    q = queries.reshape(4, GROUPS, HEADS_PER_GROUP, WIDTH).transpose(1, 2, 0, 3)
    q = q.reshape(GROUPS, 1, 64, WIDTH)
    q = jnp.broadcast_to(q, (GROUPS, 2, 64, WIDTH)).reshape(8, 64, WIDTH)
    q = lax.all_to_all(q, ("zl", "zh"), 0, 0, tiled=True)
    q = [q, *(lax.ppermute(q, "x", turned(k)) for k in (1, 2, 3))]
    pieces = []
    for s in range(4):
        piece = lax.dynamic_slice_in_dim(keys_values, (zl ^ s) * WIDTH, WIDTH, 2)
        pieces.append(lax.ppermute(piece, "zl", [(i, i ^ s) for i in range(4)]) if s else piece)
    a0 = jnp.stack(pieces)
    a1, a2, a3 = (lax.ppermute(a0, "y", turned(k)) for k in (1, 2, 3))
    swap = [(0, 1), (1, 0)]
    b0 = lax.ppermute(a0, "core", swap)
    b1 = lax.ppermute(a1, "core", swap)
    b3 = lax.ppermute(a3, "core", swap)
    b = [b0, b1, lax.ppermute(a2, "core", swap), b3]
    query_block = jnp.arange(8, dtype=jnp.int32)
    at = query_block * 32 + 31
    index = jnp.arange(256, dtype=jnp.int32)
    own_doc = jnp.sum(jnp.where(index[None] == at[:, None], doc_blocks[None], 0), axis=1)
    start = jnp.sum((doc_blocks[None] < own_doc[:, None]).astype(jnp.int32), axis=1)
    lo = jnp.clip((start - x - 128 * zh + 3) >> 2, 0, 32)
    end = 8 * (query_block + 1) - 32 * zh
    mine = jnp.stack([zl, y, core, (x == 3).astype(jnp.int32)]).astype(jnp.int32)
    scal = jnp.concatenate([lo, jnp.clip(end, 0, 32), mine, end, zh[None], x[None]]).astype(jnp.int32)

    part = attend_call(scal, q, (a0, a1, a2, a3), b)
    part = [part[0], *(lax.ppermute(part[k], "x", turned(4 - k)) for k in (1, 2, 3))]
    part = pl.pallas_call(
        merge,
        out_shape=jax.ShapeDtypeStruct((8, SLOT_ROWS, WIDTH), jnp.bfloat16),
        in_specs=[VMEM] * 4,
        out_specs=VMEM,
        compiler_params=PARAMS,
        name="merge",
    )(*part)
    part = lax.all_to_all(part, ("zl", "zh"), 0, 0, tiled=True)
    return pl.pallas_call(
        combine,
        out_shape=jax.ShapeDtypeStruct((4, HEADS * WIDTH), jnp.bfloat16),
        in_specs=[SMEM, VMEM],
        out_specs=VMEM,
        compiler_params=PARAMS,
        name="combine",
    )(scal, part)


def solution(mesh):
    split = Mesh(mesh.devices.reshape(4, 4, 2, 4, 2), ("zl", "x", "zh", "y", "core"))
    in_specs = (
        P(("zl", "x", "zh", "y", "core"), None),
        P(None, ("zh", "y", "core", "zl", "x"), None),
        P(),
    )
    out_specs = P(("zl", "x", "zh", "y", "core"), None)
    return jax.shard_map(
        per_device, mesh=split, in_specs=in_specs, out_specs=out_specs, check_vma=False
    )
```

```python
import math

import jax
import jax.numpy as jnp
from jax import lax
from jax.experimental import pallas as pl
from jax.experimental.pallas import tpu as pltpu
from jax.sharding import Mesh
from jax.sharding import PartitionSpec as P

HEADS = 64
GROUPS = 4
WIDTH = 128
BLOCK = 128
HEADS_PER_GROUP = HEADS // GROUPS
SLOT_ROWS = 72
ROWS = 256
KEYS = 1024
STEP = KEYS // BLOCK
MASKED = -1e30
EXP_SCALE = math.log2(math.e) / math.sqrt(WIDTH)
VMEM = pl.BlockSpec(memory_space=pltpu.VMEM)
SMEM = pl.BlockSpec(memory_space=pltpu.SMEM)
PARAMS = pltpu.CompilerParams(vmem_limit_bytes=32 * 1024 * 1024)


def three_pieces(value):
    hi = value.astype(jnp.bfloat16).astype(jnp.float32)
    rest = value - hi
    mid = rest.astype(jnp.bfloat16).astype(jnp.float32)
    return hi, mid, rest - mid


def statistics(m, l):
    rows = (*three_pieces(m), *three_pieces(l), jnp.zeros((2, WIDTH), jnp.float32))
    return jnp.concatenate(rows, axis=0).astype(jnp.bfloat16)


def attend(
    scal, q0, q1, q2, q3, a0, a1, a2, a3, b0, b1, b2, b3, o0, o1, o2, o3,
    q_ref, k_scr, v_scr, acc, m_scr, l_scr, steps, s_a, s_b, p_a, p_b,
):
    zl, y, core, causal = scal[16], scal[17], scal[18], scal[19]
    for k in range(4):
        own, other = (a0, a1, a2, a3)[k], (b0, b1, b2, b3)[k]
        for s in range(4):
            at = ((y + k) & 3) * 8 + (s ^ zl)
            for src, p in ((own, at + core * 4), (other, at + (core ^ 1) * 4)):
                rows = pl.ds(pl.multiple_of(p * BLOCK, BLOCK), BLOCK)
                k_scr[rows, :] = src[s, 0]
                v_scr[rows, :] = src[s, 1]
    for k in range(4):
        x_at = (scal[29] + k) & 3
        for src in range(8):
            slot = src // 2 * 8 + x_at * 2 + src % 2
            q_ref[pl.ds(pl.multiple_of(slot * 64, 64), 64), :] = (q0, q1, q2, q3)[k][src]
    m_scr[...] = jnp.full_like(m_scr, MASKED)
    l_scr[...] = jnp.zeros_like(l_scr)

    def put(n, group, start, lo, slack):
        steps[0, n] = group
        steps[1, n] = start
        steps[2, n] = lo
        steps[3, n] = slack

    def plan(group, n):
        lo, hi = scal[group], scal[8 + group]
        count = (jnp.maximum(hi - lo, 0) + STEP - 1) // STEP

        @pl.when(count > 0)
        def _():
            acc[group] = jnp.zeros((WIDTH, ROWS), jnp.float32)

        def one(i, n):
            diagonal = (i == 0) & (causal == 1) & (hi == scal[20 + group])
            put(n, group, hi - STEP - STEP * i, lo, jnp.where(diagonal, 0, BLOCK))
            return n + 1

        return lax.fori_loop(0, count, one, n)

    n = lax.fori_loop(0, 8, plan, jnp.int32(0))
    key = lax.broadcasted_iota(jnp.int32, (BLOCK, ROWS), 0)
    row = lax.broadcasted_iota(jnp.int32, (1, ROWS), 1)
    query = (row >> 7) * 64 + ((row >> 6) & 1) * 32 + y * 8 + core * 4 + (row & 3)

    def scores(i, s_ref):
        group, start = steps[0, i], steps[1, i]
        keys = k_scr[pl.ds(pl.multiple_of(start * BLOCK, KEYS), KEYS), :]
        q = q_ref[pl.ds(pl.multiple_of(group * ROWS, ROWS), ROWS), :]
        s_ref[...] = lax.dot_general(
            keys, q, (((1,), (1,)), ((), ())), preferred_element_type=jnp.float32
        )

    def weigh(i, s_ref, p_ref):
        group, start, lo, slack = steps[0, i], steps[1, i], steps[2, i], steps[3, i]
        tail = slice(KEYS - BLOCK, KEYS)
        s_ref[tail, :] = jnp.where(key <= query + slack, s_ref[tail, :], MASKED)
        m_old = m_scr[group, 0:1, :]
        m_new = m_old
        bias = []
        for j in range(STEP):
            bias.append(jnp.where(start + j < lo, jnp.float32(MASKED), jnp.float32(0.0)))
            top = jnp.max(s_ref[j * BLOCK : (j + 1) * BLOCK, :], axis=0, keepdims=True)
            m_new = jnp.maximum(m_new, top + bias[j])
        total = jnp.zeros((1, ROWS), jnp.float32)
        for j in range(STEP):
            at = slice(j * BLOCK, (j + 1) * BLOCK)
            p = jnp.exp2((s_ref[at, :] - (m_new - bias[j])) * EXP_SCALE)
            total = total + jnp.sum(p, axis=0, keepdims=True)
            p_ref[at, :] = p.astype(jnp.bfloat16)
        alpha = jnp.exp2((m_old - m_new) * EXP_SCALE)
        m_scr[group, 0:1, :] = m_new
        l_scr[group, 0:1, :] = l_scr[group, 0:1, :] * alpha + total
        values = v_scr[pl.ds(pl.multiple_of(start * BLOCK, KEYS), KEYS), :]
        acc[group] = acc[group] * alpha + lax.dot_general(
            values, p_ref[...], (((0,), (0,)), ((), ())), preferred_element_type=jnp.float32
        )

    @pl.when(n > 0)
    def _():
        for extra in range(2):
            put(n + extra, steps[0, n - 1], steps[1, n - 1], 64, BLOCK)
        scores(0, s_a)

        def pair(i, carry):
            scores(2 * i + 1, s_b)
            weigh(2 * i, s_a, p_a)
            scores(2 * i + 2, s_a)
            weigh(2 * i + 1, s_b, p_b)
            return carry

        lax.fori_loop(0, (n + 1) // 2, pair, 0)

    for k, out_ref in enumerate((o0, o1, o2, o3)):
        x_at = (scal[29] + k) & 3
        lanes = pl.ds(pl.multiple_of((x_at & 1) * 128, 128), 128)

        def finish(zl_at, carry, out_ref=out_ref, x_at=x_at, lanes=lanes):
            group = 2 * zl_at + (x_at >> 1)
            live = scal[group] < scal[8 + group]

            @pl.when(live)
            def _():
                part = acc[group, :, lanes].T.astype(jnp.bfloat16)
                for j in range(2):
                    out_ref[zl_at * 2 + j, 0:64, :] = part[j * 64 : (j + 1) * 64]

            @pl.when(jnp.logical_not(live))
            def _():
                for j in range(2):
                    out_ref[zl_at * 2 + j, 0:64, :] = jnp.zeros((64, WIDTH), jnp.bfloat16)

            stats = statistics(m_scr[group, 0:1, lanes], l_scr[group, 0:1, lanes])
            for j in range(2):
                out_ref[zl_at * 2 + j, 64:72, :] = stats
            return carry

        lax.fori_loop(0, 4, finish, 0)


def attend_call(scal, q, a, b):
    return pl.pallas_call(
        attend,
        out_shape=(jax.ShapeDtypeStruct((8, SLOT_ROWS, WIDTH), jnp.bfloat16),) * 4,
        in_specs=[SMEM] + [VMEM] * 12,
        out_specs=(VMEM,) * 4,
        scratch_shapes=[
            pltpu.VMEM((2048, WIDTH), jnp.bfloat16),
            pltpu.VMEM((32 * BLOCK, WIDTH), jnp.bfloat16),
            pltpu.VMEM((32 * BLOCK, WIDTH), jnp.bfloat16),
            pltpu.VMEM((8, WIDTH, ROWS), jnp.float32),
            pltpu.VMEM((8, 8, ROWS), jnp.float32),
            pltpu.VMEM((8, 8, ROWS), jnp.float32),
            pltpu.SMEM((4, 72), jnp.int32),
            pltpu.VMEM((KEYS, ROWS), jnp.float32),
            pltpu.VMEM((KEYS, ROWS), jnp.float32),
            pltpu.VMEM((KEYS, ROWS), jnp.bfloat16),
            pltpu.VMEM((KEYS, ROWS), jnp.bfloat16),
        ],
        compiler_params=PARAMS,
        name="attend",
    )(scal, *q, *a, *b)


def weights(stats):
    stats = [st.astype(jnp.float32) for st in stats]
    m = jnp.concatenate([st[0:1] + st[1:2] + st[2:3] for st in stats], axis=0)
    l = jnp.concatenate([st[3:4] + st[4:5] + st[5:6] for st in stats], axis=0)
    top = jnp.max(m, axis=0, keepdims=True)
    w = jnp.exp2((m - top) * EXP_SCALE)
    return top, w, jnp.sum(w * l, axis=0, keepdims=True)


def weighed(line, pick, rows):
    total = jnp.zeros((pick.shape[0], WIDTH), jnp.float32)
    for piece in three_pieces(line):
        spread = jnp.where(pick, jnp.broadcast_to(piece, pick.shape), 0.0).astype(jnp.bfloat16)
        total = total + jnp.dot(spread, rows, preferred_element_type=jnp.float32)
    return total


def merge(p0, p1, p2, p3, out_ref):
    parts = (p0, p1, p2, p3)
    pick = lax.broadcasted_iota(jnp.int32, (128, 512), 1) & 127
    pick = pick == lax.broadcasted_iota(jnp.int32, (128, 512), 0)
    for zl_at in range(4):
        top, w, l = weights([part[2 * zl_at, 64:72, :] for part in parts])
        line = jnp.concatenate([w[k : k + 1] for k in range(4)], axis=1)
        rows = [part[2 * zl_at + j, 0:64, :] for part in parts for j in range(2)]
        total = weighed(line, pick, jnp.concatenate(rows, axis=0)).astype(jnp.bfloat16)
        stats = statistics(top, l)
        for j in range(2):
            out_ref[2 * zl_at + j, 0:64, :] = total[j * 64 : (j + 1) * 64]
            out_ref[2 * zl_at + j, 64:72, :] = stats


def combine(scal, parts, out_ref):
    odd = scal[28] == 1
    lane = lax.broadcasted_iota(jnp.int32, (1, WIDTH), 1)
    pick = lax.broadcasted_iota(jnp.int32, (64, WIDTH), 1) & 63
    pick = pick == lax.broadcasted_iota(jnp.int32, (64, WIDTH), 0)
    for g in range(GROUPS):
        _, w, l = weights([parts[g * 2 + j, 64:72, :] for j in range(2)])
        w = w / l
        turned_w = pltpu.roll(w, 64, 1)
        low, high = jnp.where(odd, turned_w, w), jnp.where(odd, w, turned_w)
        line = jnp.where(lane < 64, low[0:1], high[1:2])
        rows = jnp.concatenate([parts[g * 2 + j, 0:64, :] for j in range(2)], axis=0)
        total = weighed(line, pick, rows)
        for h in range(HEADS_PER_GROUP):
            at = (g * HEADS_PER_GROUP + h) * WIDTH
            out_ref[:, at : at + WIDTH] = total[h * 4 : (h + 1) * 4, :].astype(jnp.bfloat16)


def turned(k):
    return [((i + k) % 4, i) for i in range(4)]


def per_device(queries, keys_values, doc_blocks):
    zl, x, zh, y, core = (lax.axis_index(a) for a in ("zl", "x", "zh", "y", "core"))
    q = queries.reshape(4, GROUPS, HEADS_PER_GROUP, WIDTH).transpose(1, 2, 0, 3)
    q = q.reshape(GROUPS, 1, 64, WIDTH)
    q = jnp.broadcast_to(q, (GROUPS, 2, 64, WIDTH)).reshape(8, 64, WIDTH)
    q = lax.all_to_all(q, ("zl", "zh"), 0, 0, tiled=True)
    q = [q, *(lax.ppermute(q, "x", turned(k)) for k in (1, 2, 3))]
    pieces = []
    for s in range(4):
        piece = lax.dynamic_slice_in_dim(keys_values, (zl ^ s) * WIDTH, WIDTH, 2)
        pieces.append(lax.ppermute(piece, "zl", [(i, i ^ s) for i in range(4)]) if s else piece)
    a0 = jnp.stack(pieces)
    a1, a2, a3 = (lax.ppermute(a0, "y", turned(k)) for k in (1, 2, 3))
    swap = [(0, 1), (1, 0)]
    late, a3 = lax.optimization_barrier((a0, a3))
    b = [lax.ppermute(a, "core", swap) for a in (late, a1, a2, a3)]
    query_block = jnp.arange(8, dtype=jnp.int32)
    at = query_block * 32 + 31
    index = jnp.arange(256, dtype=jnp.int32)
    own_doc = jnp.sum(jnp.where(index[None] == at[:, None], doc_blocks[None], 0), axis=1)
    start = jnp.sum((doc_blocks[None] < own_doc[:, None]).astype(jnp.int32), axis=1)
    lo = jnp.clip((start - x - 128 * zh + 3) >> 2, 0, 32)
    end = 8 * (query_block + 1) - 32 * zh
    mine = jnp.stack([zl, y, core, (x == 3).astype(jnp.int32)]).astype(jnp.int32)
    scal = jnp.concatenate([lo, jnp.clip(end, 0, 32), mine, end, zh[None], x[None]]).astype(jnp.int32)

    part = attend_call(scal, q, (a0, a1, a2, a3), b)
    part = [part[0], *(lax.ppermute(part[k], "x", turned(4 - k)) for k in (1, 2, 3))]
    part = pl.pallas_call(
        merge,
        out_shape=jax.ShapeDtypeStruct((8, SLOT_ROWS, WIDTH), jnp.bfloat16),
        in_specs=[VMEM] * 4,
        out_specs=VMEM,
        compiler_params=PARAMS,
        name="merge",
    )(*part)
    part = lax.all_to_all(part, ("zl", "zh"), 0, 0, tiled=True)
    return pl.pallas_call(
        combine,
        out_shape=jax.ShapeDtypeStruct((4, HEADS * WIDTH), jnp.bfloat16),
        in_specs=[SMEM, VMEM],
        out_specs=VMEM,
        compiler_params=PARAMS,
        name="combine",
    )(scal, part)


def solution(mesh):
    split = Mesh(mesh.devices.reshape(4, 4, 2, 4, 2), ("zl", "x", "zh", "y", "core"))
    in_specs = (
        P(("zl", "x", "zh", "y", "core"), None),
        P(None, ("zh", "y", "core", "zl", "x"), None),
        P(),
    )
    out_specs = P(("zl", "x", "zh", "y", "core"), None)
    return jax.shard_map(
        per_device, mesh=split, in_specs=in_specs, out_specs=out_specs, check_vma=False
    )
```

```python
import math

import jax
import jax.numpy as jnp
from jax import lax
from jax.experimental import pallas as pl
from jax.experimental.pallas import tpu as pltpu
from jax.sharding import Mesh
from jax.sharding import PartitionSpec as P

HEADS = 64
GROUPS = 4
WIDTH = 128
BLOCK = 128
HEADS_PER_GROUP = HEADS // GROUPS
SLOT_ROWS = 72
ROWS = 256
KEYS = 1024
STEP = KEYS // BLOCK
MASKED = -1e30
EXP_SCALE = math.log2(math.e) / math.sqrt(WIDTH)
VMEM = pl.BlockSpec(memory_space=pltpu.VMEM)
SMEM = pl.BlockSpec(memory_space=pltpu.SMEM)
PARAMS = pltpu.CompilerParams(vmem_limit_bytes=32 * 1024 * 1024)


def three_pieces(value):
    hi = value.astype(jnp.bfloat16).astype(jnp.float32)
    rest = value - hi
    mid = rest.astype(jnp.bfloat16).astype(jnp.float32)
    return hi, mid, rest - mid


def statistics(m, l):
    rows = (*three_pieces(m), *three_pieces(l), jnp.zeros((2, WIDTH), jnp.float32))
    return jnp.concatenate(rows, axis=0).astype(jnp.bfloat16)


def attend(
    scal, q0, q1, q2, q3, a0, a1, a2, a3, b0, b1, b2, b3, o0, o1, o2, o3,
    q_ref, k_scr, v_scr, acc, m_scr, l_scr, steps, s_a, s_b, p_a, p_b,
):
    zl, y, core, causal = scal[16], scal[17], scal[18], scal[19]
    for k in range(4):
        own, other = (a0, a1, a2, a3)[k], (b0, b1, b2, b3)[k]
        for s in range(4):
            at = ((y + k) & 3) * 8 + (s ^ zl)
            for src, p in ((own, at + core * 4), (other, at + (core ^ 1) * 4)):
                rows = pl.ds(pl.multiple_of(p * BLOCK, BLOCK), BLOCK)
                k_scr[rows, :] = src[s, 0]
                v_scr[rows, :] = src[s, 1]
    for k in range(4):
        x_at = (scal[29] + k) & 3
        for src in range(8):
            slot = src // 2 * 8 + x_at * 2 + src % 2
            q_ref[pl.ds(pl.multiple_of(slot * 64, 64), 64), :] = (q0, q1, q2, q3)[k][src]
    m_scr[...] = jnp.full_like(m_scr, MASKED)
    l_scr[...] = jnp.zeros_like(l_scr)

    def put(n, group, start, lo, slack):
        steps[0, n] = group
        steps[1, n] = start
        steps[2, n] = lo
        steps[3, n] = slack

    def plan(group, n):
        lo, hi = scal[group], scal[8 + group]
        count = (jnp.maximum(hi - lo, 0) + STEP - 1) // STEP

        @pl.when(count > 0)
        def _():
            acc[group] = jnp.zeros((WIDTH, ROWS), jnp.float32)

        def one(i, n):
            diagonal = (i == 0) & (causal == 1) & (hi == scal[20 + group])
            put(n, group, hi - STEP - STEP * i, lo, jnp.where(diagonal, 0, BLOCK))
            return n + 1

        return lax.fori_loop(0, count, one, n)

    n = lax.fori_loop(0, 8, plan, jnp.int32(0))
    key = lax.broadcasted_iota(jnp.int32, (BLOCK, ROWS), 0)
    row = lax.broadcasted_iota(jnp.int32, (1, ROWS), 1)
    query = (row >> 7) * 64 + ((row >> 6) & 1) * 32 + y * 8 + core * 4 + (row & 3)

    def scores(i, s_ref):
        group, start = steps[0, i], steps[1, i]
        keys = k_scr[pl.ds(pl.multiple_of(start * BLOCK, KEYS), KEYS), :]
        q = q_ref[pl.ds(pl.multiple_of(group * ROWS, ROWS), ROWS), :]
        s_ref[...] = lax.dot_general(
            keys, q, (((1,), (1,)), ((), ())), preferred_element_type=jnp.float32
        )

    def weigh(i, s_ref, p_ref):
        group, start, lo, slack = steps[0, i], steps[1, i], steps[2, i], steps[3, i]
        tail = slice(KEYS - BLOCK, KEYS)
        s_ref[tail, :] = jnp.where(key <= query + slack, s_ref[tail, :], MASKED)
        m_old = m_scr[group, 0:1, :]
        m_new = m_old
        bias = []
        for j in range(STEP):
            bias.append(jnp.where(start + j < lo, jnp.float32(MASKED), jnp.float32(0.0)))
            top = jnp.max(s_ref[j * BLOCK : (j + 1) * BLOCK, :], axis=0, keepdims=True)
            m_new = jnp.maximum(m_new, top + bias[j])
        total = jnp.zeros((1, ROWS), jnp.float32)
        for j in range(STEP):
            at = slice(j * BLOCK, (j + 1) * BLOCK)
            p = jnp.exp2((s_ref[at, :] - (m_new - bias[j])) * EXP_SCALE)
            total = total + jnp.sum(p, axis=0, keepdims=True)
            p_ref[at, :] = p.astype(jnp.bfloat16)
        alpha = jnp.exp2((m_old - m_new) * EXP_SCALE)
        m_scr[group, 0:1, :] = m_new
        l_scr[group, 0:1, :] = l_scr[group, 0:1, :] * alpha + total
        values = v_scr[pl.ds(pl.multiple_of(start * BLOCK, KEYS), KEYS), :]
        acc[group] = acc[group] * alpha + lax.dot_general(
            values, p_ref[...], (((0,), (0,)), ((), ())), preferred_element_type=jnp.float32
        )

    @pl.when(n > 0)
    def _():
        for extra in range(2):
            put(n + extra, steps[0, n - 1], steps[1, n - 1], 64, BLOCK)
        scores(0, s_a)

        def pair(i, carry):
            scores(2 * i + 1, s_b)
            weigh(2 * i, s_a, p_a)
            scores(2 * i + 2, s_a)
            weigh(2 * i + 1, s_b, p_b)
            return carry

        lax.fori_loop(0, (n + 1) // 2, pair, 0)

    for k, out_ref in enumerate((o0, o1, o2, o3)):
        x_at = (scal[29] + k) & 3
        lanes = pl.ds(pl.multiple_of((x_at & 1) * 128, 128), 128)

        def finish(zl_at, carry, out_ref=out_ref, x_at=x_at, lanes=lanes):
            group = 2 * zl_at + (x_at >> 1)
            live = scal[group] < scal[8 + group]

            @pl.when(live)
            def _():
                part = acc[group, :, lanes].T.astype(jnp.bfloat16)
                for j in range(2):
                    out_ref[zl_at * 2 + j, 0:64, :] = part[j * 64 : (j + 1) * 64]

            @pl.when(jnp.logical_not(live))
            def _():
                for j in range(2):
                    out_ref[zl_at * 2 + j, 0:64, :] = jnp.zeros((64, WIDTH), jnp.bfloat16)

            stats = statistics(m_scr[group, 0:1, lanes], l_scr[group, 0:1, lanes])
            for j in range(2):
                out_ref[zl_at * 2 + j, 64:72, :] = stats
            return carry

        lax.fori_loop(0, 4, finish, 0)


def attend_call(scal, q, a, b):
    return pl.pallas_call(
        attend,
        out_shape=(jax.ShapeDtypeStruct((8, SLOT_ROWS, WIDTH), jnp.bfloat16),) * 4,
        in_specs=[SMEM] + [VMEM] * 12,
        out_specs=(VMEM,) * 4,
        scratch_shapes=[
            pltpu.VMEM((2048, WIDTH), jnp.bfloat16),
            pltpu.VMEM((32 * BLOCK, WIDTH), jnp.bfloat16),
            pltpu.VMEM((32 * BLOCK, WIDTH), jnp.bfloat16),
            pltpu.VMEM((8, WIDTH, ROWS), jnp.float32),
            pltpu.VMEM((8, 8, ROWS), jnp.float32),
            pltpu.VMEM((8, 8, ROWS), jnp.float32),
            pltpu.SMEM((4, 72), jnp.int32),
            pltpu.VMEM((KEYS, ROWS), jnp.float32),
            pltpu.VMEM((KEYS, ROWS), jnp.float32),
            pltpu.VMEM((KEYS, ROWS), jnp.bfloat16),
            pltpu.VMEM((KEYS, ROWS), jnp.bfloat16),
        ],
        compiler_params=PARAMS,
        name="attend",
    )(scal, *q, *a, *b)


def weights(stats):
    stats = [st.astype(jnp.float32) for st in stats]
    m = jnp.concatenate([st[0:1] + st[1:2] + st[2:3] for st in stats], axis=0)
    l = jnp.concatenate([st[3:4] + st[4:5] + st[5:6] for st in stats], axis=0)
    top = jnp.max(m, axis=0, keepdims=True)
    w = jnp.exp2((m - top) * EXP_SCALE)
    return top, w, jnp.sum(w * l, axis=0, keepdims=True)


def weighed(line, pick, rows):
    total = jnp.zeros((pick.shape[0], WIDTH), jnp.float32)
    for piece in three_pieces(line):
        spread = jnp.where(pick, jnp.broadcast_to(piece, pick.shape), 0.0).astype(jnp.bfloat16)
        total = total + jnp.dot(spread, rows, preferred_element_type=jnp.float32)
    return total


def merge(p0, p1, p2, p3, out_ref):
    parts = (p0, p1, p2, p3)
    pick = lax.broadcasted_iota(jnp.int32, (128, 512), 1) & 127
    pick = pick == lax.broadcasted_iota(jnp.int32, (128, 512), 0)
    for zl_at in range(4):
        top, w, l = weights([part[2 * zl_at, 64:72, :] for part in parts])
        line = jnp.concatenate([w[k : k + 1] for k in range(4)], axis=1)
        rows = [part[2 * zl_at + j, 0:64, :] for part in parts for j in range(2)]
        total = weighed(line, pick, jnp.concatenate(rows, axis=0)).astype(jnp.bfloat16)
        stats = statistics(top, l)
        for j in range(2):
            out_ref[2 * zl_at + j, 0:64, :] = total[j * 64 : (j + 1) * 64]
            out_ref[2 * zl_at + j, 64:72, :] = stats


def combine(scal, parts, out_ref):
    odd = scal[28] == 1
    lane = lax.broadcasted_iota(jnp.int32, (1, WIDTH), 1)
    pick = lax.broadcasted_iota(jnp.int32, (64, WIDTH), 1) & 63
    pick = pick == lax.broadcasted_iota(jnp.int32, (64, WIDTH), 0)
    for g in range(GROUPS):
        _, w, l = weights([parts[g * 2 + j, 64:72, :] for j in range(2)])
        w = w / l
        turned_w = pltpu.roll(w, 64, 1)
        low, high = jnp.where(odd, turned_w, w), jnp.where(odd, w, turned_w)
        line = jnp.where(lane < 64, low[0:1], high[1:2])
        rows = jnp.concatenate([parts[g * 2 + j, 0:64, :] for j in range(2)], axis=0)
        total = weighed(line, pick, rows)
        for h in range(HEADS_PER_GROUP):
            at = (g * HEADS_PER_GROUP + h) * WIDTH
            out_ref[:, at : at + WIDTH] = total[h * 4 : (h + 1) * 4, :].astype(jnp.bfloat16)


def turned(k):
    return [((i + k) % 4, i) for i in range(4)]


def per_device(queries, keys_values, doc_blocks):
    zl, x, zh, y, core = (lax.axis_index(a) for a in ("zl", "x", "zh", "y", "core"))
    q = queries.reshape(4, GROUPS, HEADS_PER_GROUP, WIDTH).transpose(1, 2, 0, 3)
    q = q.reshape(GROUPS, 1, 64, WIDTH)
    q = jnp.broadcast_to(q, (GROUPS, 2, 64, WIDTH)).reshape(8, 64, WIDTH)
    q = lax.all_to_all(q, ("zl", "zh"), 0, 0, tiled=True)
    q = [q, *(lax.ppermute(q, "x", turned(k)) for k in (1, 2, 3))]
    pieces = []
    source = keys_values
    for s in (1, 2, 3, 0):
        piece = lax.dynamic_slice_in_dim(source, (zl ^ s) * WIDTH, WIDTH, 2)
        piece, source = lax.optimization_barrier((piece, source))
        pieces.append(lax.ppermute(piece, "zl", [(i, i ^ s) for i in range(4)]) if s else piece)
    pieces = [pieces[3], *pieces[:3]]
    a0 = jnp.stack(pieces)
    a1, a2, a3 = (lax.ppermute(a0, "y", turned(k)) for k in (1, 2, 3))
    swap = [(0, 1), (1, 0)]
    late, a3 = lax.optimization_barrier((a0, a3))
    b = [lax.ppermute(a, "core", swap) for a in (late, a1, a2, a3)]
    query_block = jnp.arange(8, dtype=jnp.int32)
    at = query_block * 32 + 31
    index = jnp.arange(256, dtype=jnp.int32)
    own_doc = jnp.sum(jnp.where(index[None] == at[:, None], doc_blocks[None], 0), axis=1)
    start = jnp.sum((doc_blocks[None] < own_doc[:, None]).astype(jnp.int32), axis=1)
    lo = jnp.clip((start - x - 128 * zh + 3) >> 2, 0, 32)
    end = 8 * (query_block + 1) - 32 * zh
    mine = jnp.stack([zl, y, core, (x == 3).astype(jnp.int32)]).astype(jnp.int32)
    scal = jnp.concatenate([lo, jnp.clip(end, 0, 32), mine, end, zh[None], x[None]]).astype(jnp.int32)

    part = attend_call(scal, q, (a0, a1, a2, a3), b)
    part = [part[0], *(lax.ppermute(part[k], "x", turned(4 - k)) for k in (1, 2, 3))]
    part = pl.pallas_call(
        merge,
        out_shape=jax.ShapeDtypeStruct((8, SLOT_ROWS, WIDTH), jnp.bfloat16),
        in_specs=[VMEM] * 4,
        out_specs=VMEM,
        compiler_params=PARAMS,
        name="merge",
    )(*part)
    part = lax.all_to_all(part, ("zl", "zh"), 0, 0, tiled=True)
    return pl.pallas_call(
        combine,
        out_shape=jax.ShapeDtypeStruct((4, HEADS * WIDTH), jnp.bfloat16),
        in_specs=[SMEM, VMEM],
        out_specs=VMEM,
        compiler_params=PARAMS,
        name="combine",
    )(scal, part)


def solution(mesh):
    split = Mesh(mesh.devices.reshape(4, 4, 2, 4, 2), ("zl", "x", "zh", "y", "core"))
    in_specs = (
        P(("zl", "x", "zh", "y", "core"), None),
        P(None, ("zh", "y", "core", "zl", "x"), None),
        P(),
    )
    out_specs = P(("zl", "x", "zh", "y", "core"), None)
    return jax.shard_map(
        per_device, mesh=split, in_specs=in_specs, out_specs=out_specs, check_vma=False
    )
```

```python
import math

import jax
import jax.numpy as jnp
from jax import lax
from jax.experimental import pallas as pl
from jax.experimental.pallas import tpu as pltpu
from jax.sharding import Mesh
from jax.sharding import PartitionSpec as P

HEADS = 64
GROUPS = 4
WIDTH = 128
BLOCK = 128
HEADS_PER_GROUP = HEADS // GROUPS
SLOT_ROWS = 72
ROWS = 256
KEYS = 1024
STEP = KEYS // BLOCK
MASKED = -1e30
EXP_SCALE = math.log2(math.e) / math.sqrt(WIDTH)
VMEM = pl.BlockSpec(memory_space=pltpu.VMEM)
SMEM = pl.BlockSpec(memory_space=pltpu.SMEM)
PARAMS = pltpu.CompilerParams(vmem_limit_bytes=32 * 1024 * 1024)


def three_pieces(value):
    hi = value.astype(jnp.bfloat16).astype(jnp.float32)
    rest = value - hi
    mid = rest.astype(jnp.bfloat16).astype(jnp.float32)
    return hi, mid, rest - mid


def statistics(m, l):
    rows = (*three_pieces(m), *three_pieces(l), jnp.zeros((2, WIDTH), jnp.float32))
    return jnp.concatenate(rows, axis=0).astype(jnp.bfloat16)


def attend(
    scal, q0, q1, q2, q3, a0, a1, a2, a3, b0, b1, b2, b3, o0, o1, o2, o3,
    q_ref, k_scr, v_scr, acc, m_scr, l_scr, steps, s_a, s_b, p_a, p_b,
):
    zl, y, core, causal = scal[16], scal[17], scal[18], scal[19]
    for k in range(4):
        own, other = (a0, a1, a2, a3)[k], (b0, b1, b2, b3)[k]
        for s in range(4):
            at = ((y + k) & 3) * 8 + (s ^ zl)
            for src, p in ((own, at + core * 4), (other, at + (core ^ 1) * 4)):
                rows = pl.ds(pl.multiple_of(p * BLOCK, BLOCK), BLOCK)
                k_scr[rows, :] = src[s, 0]
                v_scr[rows, :] = src[s, 1]
    for k in range(4):
        x_at = (scal[29] + k) & 3
        for src in range(8):
            slot = src // 2 * 8 + x_at * 2 + src % 2
            q_ref[pl.ds(pl.multiple_of(slot * 64, 64), 64), :] = (q0, q1, q2, q3)[k][src]
    m_scr[...] = jnp.full_like(m_scr, MASKED)
    l_scr[...] = jnp.zeros_like(l_scr)

    def put(n, group, start, lo, slack):
        steps[0, n] = group
        steps[1, n] = start
        steps[2, n] = lo
        steps[3, n] = slack

    def plan(group, n):
        lo, hi = scal[group], scal[8 + group]
        count = (jnp.maximum(hi - lo, 0) + STEP - 1) // STEP

        @pl.when(count > 0)
        def _():
            acc[group] = jnp.zeros((WIDTH, ROWS), jnp.float32)

        def one(i, n):
            diagonal = (i == 0) & (causal == 1) & (hi == scal[20 + group])
            put(n, group, hi - STEP - STEP * i, lo, jnp.where(diagonal, 0, BLOCK))
            return n + 1

        return lax.fori_loop(0, count, one, n)

    n = lax.fori_loop(0, 8, plan, jnp.int32(0))
    key = lax.broadcasted_iota(jnp.int32, (BLOCK, ROWS), 0)
    row = lax.broadcasted_iota(jnp.int32, (1, ROWS), 1)
    query = (row >> 7) * 64 + ((row >> 6) & 1) * 32 + y * 8 + core * 4 + (row & 3)

    def scores(i, s_ref):
        group, start = steps[0, i], steps[1, i]
        keys = k_scr[pl.ds(pl.multiple_of(start * BLOCK, KEYS), KEYS), :]
        q = q_ref[pl.ds(pl.multiple_of(group * ROWS, ROWS), ROWS), :]
        s_ref[...] = lax.dot_general(
            keys, q, (((1,), (1,)), ((), ())), preferred_element_type=jnp.float32
        )

    def weigh(i, s_ref, p_ref):
        group, start, lo, slack = steps[0, i], steps[1, i], steps[2, i], steps[3, i]
        tail = slice(KEYS - BLOCK, KEYS)
        s_ref[tail, :] = jnp.where(key <= query + slack, s_ref[tail, :], MASKED)
        m_old = m_scr[group, 0:1, :]
        m_new = m_old
        bias = []
        for j in range(STEP):
            bias.append(jnp.where(start + j < lo, jnp.float32(MASKED), jnp.float32(0.0)))
            top = jnp.max(s_ref[j * BLOCK : (j + 1) * BLOCK, :], axis=0, keepdims=True)
            m_new = jnp.maximum(m_new, top + bias[j])
        total = jnp.zeros((1, ROWS), jnp.float32)
        for j in range(STEP):
            at = slice(j * BLOCK, (j + 1) * BLOCK)
            p = jnp.exp2((s_ref[at, :] - (m_new - bias[j])) * EXP_SCALE)
            total = total + jnp.sum(p, axis=0, keepdims=True)
            p_ref[at, :] = p.astype(jnp.bfloat16)
        alpha = jnp.exp2((m_old - m_new) * EXP_SCALE)
        m_scr[group, 0:1, :] = m_new
        l_scr[group, 0:1, :] = l_scr[group, 0:1, :] * alpha + total
        values = v_scr[pl.ds(pl.multiple_of(start * BLOCK, KEYS), KEYS), :]
        acc[group] = acc[group] * alpha + lax.dot_general(
            values, p_ref[...], (((0,), (0,)), ((), ())), preferred_element_type=jnp.float32
        )

    @pl.when(n > 0)
    def _():
        for extra in range(2):
            put(n + extra, steps[0, n - 1], steps[1, n - 1], 64, BLOCK)
        scores(0, s_a)

        def pair(i, carry):
            scores(2 * i + 1, s_b)
            weigh(2 * i, s_a, p_a)
            scores(2 * i + 2, s_a)
            weigh(2 * i + 1, s_b, p_b)
            return carry

        lax.fori_loop(0, (n + 1) // 2, pair, 0)

    for k, out_ref in enumerate((o0, o1, o2, o3)):
        x_at = (scal[29] + k) & 3
        lanes = pl.ds(pl.multiple_of((x_at & 1) * 128, 128), 128)

        def finish(zl_at, carry, out_ref=out_ref, x_at=x_at, lanes=lanes):
            group = 2 * zl_at + (x_at >> 1)
            live = scal[group] < scal[8 + group]

            @pl.when(live)
            def _():
                part = acc[group, :, lanes].T.astype(jnp.bfloat16)
                for j in range(2):
                    out_ref[zl_at * 2 + j, 0:64, :] = part[j * 64 : (j + 1) * 64]

            @pl.when(jnp.logical_not(live))
            def _():
                for j in range(2):
                    out_ref[zl_at * 2 + j, 0:64, :] = jnp.zeros((64, WIDTH), jnp.bfloat16)

            stats = statistics(m_scr[group, 0:1, lanes], l_scr[group, 0:1, lanes])
            for j in range(2):
                out_ref[zl_at * 2 + j, 64:72, :] = stats
            return carry

        lax.fori_loop(0, 4, finish, 0)


def attend_call(scal, q, a, b):
    return pl.pallas_call(
        attend,
        out_shape=(jax.ShapeDtypeStruct((8, SLOT_ROWS, WIDTH), jnp.bfloat16),) * 4,
        in_specs=[SMEM] + [VMEM] * 12,
        out_specs=(VMEM,) * 4,
        scratch_shapes=[
            pltpu.VMEM((2048, WIDTH), jnp.bfloat16),
            pltpu.VMEM((32 * BLOCK, WIDTH), jnp.bfloat16),
            pltpu.VMEM((32 * BLOCK, WIDTH), jnp.bfloat16),
            pltpu.VMEM((8, WIDTH, ROWS), jnp.float32),
            pltpu.VMEM((8, 8, ROWS), jnp.float32),
            pltpu.VMEM((8, 8, ROWS), jnp.float32),
            pltpu.SMEM((4, 72), jnp.int32),
            pltpu.VMEM((KEYS, ROWS), jnp.float32),
            pltpu.VMEM((KEYS, ROWS), jnp.float32),
            pltpu.VMEM((KEYS, ROWS), jnp.bfloat16),
            pltpu.VMEM((KEYS, ROWS), jnp.bfloat16),
        ],
        compiler_params=PARAMS,
        name="attend",
    )(scal, *q, *a, *b)


def weights(stats):
    stats = [st.astype(jnp.float32) for st in stats]
    m = jnp.concatenate([st[0:1] + st[1:2] + st[2:3] for st in stats], axis=0)
    l = jnp.concatenate([st[3:4] + st[4:5] + st[5:6] for st in stats], axis=0)
    top = jnp.max(m, axis=0, keepdims=True)
    w = jnp.exp2((m - top) * EXP_SCALE)
    return top, w, jnp.sum(w * l, axis=0, keepdims=True)


def weighed(line, pick, rows):
    total = jnp.zeros((pick.shape[0], WIDTH), jnp.float32)
    for piece in three_pieces(line)[:2]:
        spread = jnp.where(pick, jnp.broadcast_to(piece, pick.shape), 0.0).astype(jnp.bfloat16)
        total = total + jnp.dot(spread, rows, preferred_element_type=jnp.float32)
    return total


def merge(p0, p1, p2, p3, out_ref):
    parts = (p0, p1, p2, p3)
    pick = lax.broadcasted_iota(jnp.int32, (128, 512), 1) & 127
    pick = pick == lax.broadcasted_iota(jnp.int32, (128, 512), 0)
    for zl_at in range(4):
        top, w, l = weights([part[2 * zl_at, 64:72, :] for part in parts])
        line = jnp.concatenate([w[k : k + 1] for k in range(4)], axis=1)
        rows = [part[2 * zl_at + j, 0:64, :] for part in parts for j in range(2)]
        total = weighed(line, pick, jnp.concatenate(rows, axis=0)).astype(jnp.bfloat16)
        stats = statistics(top, l)
        for j in range(2):
            out_ref[2 * zl_at + j, 0:64, :] = total[j * 64 : (j + 1) * 64]
            out_ref[2 * zl_at + j, 64:72, :] = stats


def combine(scal, parts, out_ref):
    odd = scal[28] == 1
    lane = lax.broadcasted_iota(jnp.int32, (1, WIDTH), 1)
    pick = lax.broadcasted_iota(jnp.int32, (64, WIDTH), 1) & 63
    pick = pick == lax.broadcasted_iota(jnp.int32, (64, WIDTH), 0)
    for g in range(GROUPS):
        _, w, l = weights([parts[g * 2 + j, 64:72, :] for j in range(2)])
        w = w / l
        turned_w = pltpu.roll(w, 64, 1)
        low, high = jnp.where(odd, turned_w, w), jnp.where(odd, w, turned_w)
        line = jnp.where(lane < 64, low[0:1], high[1:2])
        rows = jnp.concatenate([parts[g * 2 + j, 0:64, :] for j in range(2)], axis=0)
        total = weighed(line, pick, rows)
        for h in range(HEADS_PER_GROUP):
            at = (g * HEADS_PER_GROUP + h) * WIDTH
            out_ref[:, at : at + WIDTH] = total[h * 4 : (h + 1) * 4, :].astype(jnp.bfloat16)


def turned(k):
    return [((i + k) % 4, i) for i in range(4)]


def per_device(queries, keys_values, doc_blocks):
    zl, x, zh, y, core = (lax.axis_index(a) for a in ("zl", "x", "zh", "y", "core"))
    q = queries.reshape(4, GROUPS, HEADS_PER_GROUP, WIDTH).transpose(1, 2, 0, 3)
    q = q.reshape(GROUPS, 1, 64, WIDTH)
    q = jnp.broadcast_to(q, (GROUPS, 2, 64, WIDTH)).reshape(8, 64, WIDTH)
    q = lax.all_to_all(q, ("zl", "zh"), 0, 0, tiled=True)
    q = [q, *(lax.ppermute(q, "x", turned(k)) for k in (1, 2, 3))]
    pieces = []
    source = keys_values
    for s in (1, 2, 3, 0):
        piece = lax.dynamic_slice_in_dim(source, (zl ^ s) * WIDTH, WIDTH, 2)
        piece, source = lax.optimization_barrier((piece, source))
        pieces.append(lax.ppermute(piece, "zl", [(i, i ^ s) for i in range(4)]) if s else piece)
    pieces = [pieces[3], *pieces[:3]]
    a0 = jnp.stack(pieces)
    a1, a2, a3 = (lax.ppermute(a0, "y", turned(k)) for k in (1, 2, 3))
    swap = [(0, 1), (1, 0)]
    late, a3 = lax.optimization_barrier((a0, a3))
    b = [lax.ppermute(a, "core", swap) for a in (late, a1, a2, a3)]
    query_block = jnp.arange(8, dtype=jnp.int32)
    at = query_block * 32 + 31
    index = jnp.arange(256, dtype=jnp.int32)
    own_doc = jnp.sum(jnp.where(index[None] == at[:, None], doc_blocks[None], 0), axis=1)
    start = jnp.sum((doc_blocks[None] < own_doc[:, None]).astype(jnp.int32), axis=1)
    lo = jnp.clip((start - x - 128 * zh + 3) >> 2, 0, 32)
    end = 8 * (query_block + 1) - 32 * zh
    mine = jnp.stack([zl, y, core, (x == 3).astype(jnp.int32)]).astype(jnp.int32)
    scal = jnp.concatenate([lo, jnp.clip(end, 0, 32), mine, end, zh[None], x[None]]).astype(jnp.int32)

    part = attend_call(scal, q, (a0, a1, a2, a3), b)
    part = [part[0], *(lax.ppermute(part[k], "x", turned(4 - k)) for k in (1, 2, 3))]
    part = pl.pallas_call(
        merge,
        out_shape=jax.ShapeDtypeStruct((8, SLOT_ROWS, WIDTH), jnp.bfloat16),
        in_specs=[VMEM] * 4,
        out_specs=VMEM,
        compiler_params=PARAMS,
        name="merge",
    )(*part)
    part = lax.all_to_all(part, ("zl", "zh"), 0, 0, tiled=True)
    return pl.pallas_call(
        combine,
        out_shape=jax.ShapeDtypeStruct((4, HEADS * WIDTH), jnp.bfloat16),
        in_specs=[SMEM, VMEM],
        out_specs=VMEM,
        compiler_params=PARAMS,
        name="combine",
    )(scal, part)


def solution(mesh):
    split = Mesh(mesh.devices.reshape(4, 4, 2, 4, 2), ("zl", "x", "zh", "y", "core"))
    in_specs = (
        P(("zl", "x", "zh", "y", "core"), None),
        P(None, ("zh", "y", "core", "zl", "x"), None),
        P(),
    )
    out_specs = P(("zl", "x", "zh", "y", "core"), None)
    return jax.shard_map(
        per_device, mesh=split, in_specs=in_specs, out_specs=out_specs, check_vma=False
    )
```
